32 devices in a mesh: row: 2 (over x), col: 16 (over z, y, core).
Axes of the slice: x: 2, y: 2, z: 4, core: 2. Of those that a mesh axis runs over, the one named last changes fastest.
Arguments:
- contexts: bfloat16 [4096, 128], P(('row', 'col')), may hold values from -8 to 8
- logged_actions: int32 [4096], P(('row', 'col')), may hold values from 0 to 131041
- policy_actions: int32 [4096, 8], P(('row', 'col')), may hold values from 0 to 131041
- rewards: float32 [4096], P(('row', 'col')), may hold values from 0.2 to 2
Outputs:
- weights: float32 [4096, 8], P(('row', 'col'))
- residual: float32 [4096, 8], P(('row', 'col'))
- values: float32 [8], replicated
The draws below stay inside these ranges and needn't reach their ends.
All inputs are finite; a program needn't handle non-finite values.
Results may differ from the reference program's by a relative error of at most 0.0056.
Values may be sent and summed in bfloat16 or wider, within the bound.
A program may use at most 64 MiB of HBM per device.

```python
import math
import jax
import jax.numpy as jnp
from jax import lax

D = 128
NPOL = 8
NACT = 16
CATALOG = 131042
TOTAL = 4096


latent_dims = 8


def draw_contexts(key, part):
    latent_key, jitter_key, coef_key, rough_key = jax.random.split(key, 4)
    latent = jnp.clip(jax.random.normal(latent_key, (TOTAL, latent_dims), jnp.float32), -3.0, 3.0)
    fine_jitter = jnp.clip(jax.random.normal(jitter_key, (TOTAL, D), jnp.float32), -4.0, 4.0)
    coefficients = jax.random.uniform(coef_key, (D,), jnp.float32, 1.0, 1.7)
    feature_latent = jnp.arange(D, dtype=jnp.int32) % latent_dims
    spread = latent[:, feature_latent] * coefficients[None, :] + 0.3 * fine_jitter
    ramp_scale = 0.6 + 0.6 * jnp.arange(TOTAL, dtype=jnp.float32) / TOTAL
    roughness = jnp.exp(jax.random.uniform(rough_key, (TOTAL,), jnp.float32, -0.1, 0.1))
    placed = spread * (ramp_scale * roughness)[:, None]
    return jnp.clip(placed, -7.9, 7.9).astype(jnp.bfloat16)


def draw_logged_actions(key, part):
    own_key = jax.random.fold_in(key, 11)
    drawn = jax.random.randint(own_key, (TOTAL,), 0, CATALOG, dtype=jnp.int32)
    return drawn.at[0].set(0).at[TOTAL - 1].set(CATALOG - 1).astype(jnp.int32)


def draw_policy_actions(key, part):
    own_key = jax.random.fold_in(key, 23)
    drawn = jax.random.randint(own_key, (TOTAL, NPOL), 0, CATALOG, dtype=jnp.int32)
    return drawn.at[0, 0].set(0).at[TOTAL - 1, NPOL - 1].set(CATALOG - 1).astype(jnp.int32)


def shard_levels(rng, shape, pieces, least, largest):
    factor_of, own = 1.0, jax.random.fold_in(rng, 6)
    for axis_at, shards_of in pieces:
        heights = jnp.exp(jax.random.uniform(jax.random.fold_in(own, axis_at), (shards_of,), jnp.float32, least / len(pieces), largest / len(pieces)))
        factor_of = factor_of * jnp.repeat(heights, shape[axis_at] // shards_of).reshape([-1 if axis == axis_at else 1 for axis in range(len(shape))])
    return factor_of


def setup_inputs(seed: int = 0) -> dict:
    key_list = jax.random.split(jax.random.key(seed), 5)
    contexts = draw_contexts(jax.random.fold_in(key_list[4], 71), 0)
    logged_actions = draw_logged_actions(jax.random.fold_in(key_list[4], 71), 0)
    policy_actions = draw_policy_actions(jax.random.fold_in(key_list[4], 71), 0)
    rewards = jnp.clip(jnp.exp(math.log(2.0) - 2.3025851 * jax.random.uniform(key_list[3], (TOTAL,), jnp.float32) ** shard_levels(key_list[3], (TOTAL,), ((0, 32),), -0.2, 0.2)), 0.2, 2.0)
    return dict(contexts=contexts, logged_actions=logged_actions, policy_actions=policy_actions, rewards=rewards)


ridge = 0.1
stride_base = 1009
phase_step = 0.37
two_pi = 2.0 * math.pi

def action_features(chosen, width):
    levels = jnp.arange(width, dtype=jnp.int32)
    multipliers = 1 + stride_base * levels
    turned = chosen[..., None].astype(jnp.int32) * multipliers % CATALOG
    angles = turned.astype(jnp.float32) * (two_pi / CATALOG) + phase_step * levels.astype(jnp.float32)
    wave_terms = math.sqrt(2.0 / width) * jnp.cos(angles)
    constant_term = jnp.full(wave_terms.shape, 1.0 / math.sqrt(width), jnp.float32)
    return jnp.where(levels == 0, constant_term, wave_terms).astype(jnp.bfloat16)

def select_actions(products, onehot):
    shaped = products.reshape(products.shape[:-1] + (products.shape[-1] // onehot.shape[-1], onehot.shape[-1]))
    return lax.optimization_barrier(jnp.sum(shaped * jnp.expand_dims(onehot.astype(jnp.float32), -2), axis=-1))

def kernel_rows(block, everything, block_sq, all_squares):
    inner = jnp.dot(block, everything.T, preferred_element_type=jnp.float32)
    return jnp.exp((2.0 * inner - block_sq[:, None] - all_squares[None, :]) / everything.shape[1]).astype(jnp.bfloat16)

def reference(contexts, logged_actions, policy_actions, rewards):
    factor = NACT / TOTAL
    squares = lax.optimization_barrier(jnp.sum(contexts.astype(jnp.float32) ** 2, axis=1))
    logged_onehot = action_features(logged_actions, NACT)
    policy_onehot = action_features(policy_actions, NACT).reshape(TOTAL, NPOL * NACT)
    step_rows = 512
    blocks = TOTAL // step_rows
    context_blocks = contexts.reshape(blocks, step_rows, D)
    square_blocks = squares.reshape(blocks, step_rows)
    onehot_blocks = logged_onehot.reshape(blocks, step_rows, NACT)

    def first_sweep(block_args):
        block, block_sq, block_onehot = block_args
        kernel = kernel_rows(block, contexts, block_sq, squares)
        return factor * select_actions(jnp.dot(kernel, policy_onehot, preferred_element_type=jnp.float32), block_onehot)
    right_side = lax.map(first_sweep, (context_blocks, square_blocks, onehot_blocks)).reshape(TOTAL, NPOL)
    right_low = right_side.astype(jnp.bfloat16)
    matched = (logged_onehot[:, None, :] * right_low[:, :, None]).astype(jnp.bfloat16).reshape(TOTAL, NPOL * NACT)
    right_blocks = right_side.reshape(blocks, step_rows, NPOL)

    def second_sweep(block_args):
        block, block_sq, block_onehot, block_right = block_args
        kernel = kernel_rows(block, contexts, block_sq, squares)
        applied = select_actions(jnp.dot(kernel, matched, preferred_element_type=jnp.float32), block_onehot)
        return factor * applied + ridge * block_right
    image = lax.map(second_sweep, (context_blocks, square_blocks, onehot_blocks, right_blocks)).reshape(TOTAL, NPOL)
    norm_sums = lax.optimization_barrier(jnp.sum(right_side * right_side, axis=0))
    curvature = lax.optimization_barrier(jnp.sum(right_side * image, axis=0))
    reward_sums = lax.optimization_barrier(jnp.sum(rewards[:, None] * right_side, axis=0))
    alpha = norm_sums / curvature
    weights = alpha[None, :] * right_side
    residual = right_side - alpha[None, :] * image
    values = alpha * reward_sums / TOTAL
    return (weights, residual, values)
```

```python
import functools
import math

import jax
import jax.numpy as jnp
from jax import lax
from jax.experimental import pallas as pl
from jax.experimental.pallas import tpu as pltpu
from jax.sharding import PartitionSpec as P

MESH = pl.DeviceIdType.MESH
F32 = jnp.float32
BF16 = jnp.bfloat16

NPOL = 8
NACT = 16
CATALOG = 131042
RIDGE = 0.1
STRIDE = 1009
PHASE = 0.37
TWO_PI = 2.0 * math.pi
META = 32


def loop(low, high, body):
    if isinstance(low, int) and isinstance(high, int) and high - low <= 4:
        for step in range(low, high):
            body(step)
    else:

        def wrapped(step, carried):
            body(step)
            return carried

        lax.fori_loop(low, high, wrapped, 0)


def cosine(turned, phase):
    whole = jnp.floor(turned.astype(F32) * (1.0 / CATALOG) + 0.5).astype(jnp.int32)
    rest = (turned - whole * CATALOG).astype(F32)
    turns = rest * (1.0 / CATALOG) + phase / TWO_PI
    turns = turns - jnp.floor(turns + 0.5)
    angle = TWO_PI * (0.25 - jnp.abs(turns))
    square = angle * angle
    series = -1.0 / 39916800.0
    for term in (362880.0, -5040.0, 120.0, -6.0, 1.0):
        series = series * square + 1.0 / term
    return series * angle


def features(chosen):
    twice = 2.0 * cosine(chosen * STRIDE, PHASE)
    before = cosine(chosen, 0.0)
    now = cosine(chosen * (1 + STRIDE), PHASE)
    scale = math.sqrt(2.0 / NACT)
    out = [jnp.full(chosen.shape, 1.0 / math.sqrt(NACT), F32)]
    for level in range(1, NACT):
        out.append(scale * now)
        before, now = now, twice * now - before
    return out


def rounded(parts):
    return jnp.concatenate(parts, axis=0).astype(BF16)


def nt_dot(left, right):
    return lax.dot_general(left, right, (((1,), (1,)), ((), ())), preferred_element_type=F32)


def kernel(
    sizes,
    ctx_ref,
    logged_ref,
    policy_ref,
    reward_ref,
    weights_ref,
    residual_ref,
    values_ref,
    blocks,
    sides,
    grams,
    logged_feat,
    total,
    square_part,
    slots,
    block_send,
    block_recv,
    side_send,
    side_recv,
    sum_send,
    sum_recv,
):
    rows_n, depth, width = sizes
    half = rows_n * width * depth
    count = 2 * half
    rows, dims = ctx_ref.shape
    x = lax.axis_index("row")
    col = lax.axis_index("col")
    core = col % 2
    y = (col // 2) % width
    z = col // (2 * width)
    if rows_n == width:
        n1 = n2 = width
    else:
        n1 = width + core * (rows_n - width)
        n2 = rows_n + core * (width - rows_n)
    i1 = y + core * (x - y)
    i2 = x + core * (y - x)
    own_half = core * half
    own_group = i2 * n1 + i1
    me = own_half + own_group * depth + z

    def device(first, second, at_z, at_core):
        at_x = second + core * (first - second)
        at_y = first + core * (second - first)
        return (at_x, (at_z * width + at_y) * 2 + at_core)

    def z_peer(step):
        return device(i1, i2, (z + step) % depth, core)

    def first_peer(step):
        return device((i1 + step) % n1, i2, z, core)

    def second_peer(step):
        return device(i1, (i2 + step) % n2, z, core)

    core_peer = (x, (z * width + y) * 2 + 1 - core)

    barrier = pltpu.get_barrier_semaphore()

    def greet(peer):
        pl.semaphore_signal(barrier, inc=1, device_id=peer, device_id_type=MESH)

    loop(1, depth, lambda step: greet(z_peer(step)))
    loop(1, n1, lambda step: greet(first_peer(step)))
    loop(1, n2, lambda step: greet(second_peer(step)))
    greet(core_peer)

    own = ctx_ref[...]
    own_wide = own.astype(F32)
    own_squares = jnp.sum(own_wide * own_wide, axis=1, keepdims=True) * (1.0 / dims)
    square_part[...] = jnp.zeros_like(square_part)
    square_part[:, 0:NPOL] = policy_ref[...].astype(F32)
    square_part[:, NPOL : NPOL + 1] = own_squares
    turned = square_part[...].T
    chosen = turned[0:NPOL]
    squares_row = turned[NPOL : NPOL + 1]
    logged = logged_ref[...].astype(F32)

    def pieces(value):
        high = jnp.floor(value * (1.0 / 512.0) + 0.5)
        return high, value - 512.0 * high

    policy_high, policy_low = pieces(chosen)
    logged_high, logged_low = pieces(logged)
    square_1 = squares_row.astype(BF16).astype(F32)
    square_2 = (squares_row - square_1).astype(BF16).astype(F32)
    square_3 = squares_row - square_1 - square_2
    meta = jnp.concatenate(
        [
            policy_high,
            policy_low,
            jnp.broadcast_to(logged_high, (8, rows)),
            logged_low,
            square_1,
            square_2,
            square_3,
            jnp.zeros((4, rows), F32),
        ],
        axis=0,
    )
    blocks[me, 0:rows, :] = own
    blocks[me, rows : rows + META, :] = meta.astype(BF16)
    own_feat = [
        part.astype(BF16).astype(F32)
        for part in features(jnp.broadcast_to(logged_ref[...], (NPOL, rows)))
    ]

    peers = (depth - 1) + (n1 - 1) + (n2 - 1) + 1
    pl.semaphore_wait(barrier, peers)

    def spread(buffer, send_sem, recv_sem, use_group):
        def copy(index, peer):
            return pltpu.make_async_remote_copy(
                src_ref=buffer.at[index],
                dst_ref=buffer.at[index],
                send_sem=send_sem,
                recv_sem=recv_sem.at[index],
                device_id=peer,
                device_id_type=MESH,
            )

        def to_first(index):
            loop(1, n1, lambda step: copy(index, first_peer(step)).start())

        def to_second(index):
            loop(1, n2, lambda step: copy(index, second_peer(step)).start())

        def to_core(index):
            copy(index, core_peer).start()

        def arrive(index):
            copy(index, core_peer).wait_recv()

        loop(1, depth, lambda step: copy(me, z_peer(step)).start())
        to_first(me)
        to_second(me)
        to_core(me)

        def from_z(step):
            index = own_half + own_group * depth + (z + step) % depth
            arrive(index)
            to_first(index)
            to_second(index)
            to_core(index)

        loop(1, depth, from_z)
        use_group(own_half // depth + own_group)

        def from_first(step):
            group = i2 * n1 + (i1 + step) % n1

            def one(place):
                index = own_half + group * depth + place
                arrive(index)
                to_second(index)
                to_core(index)

            loop(0, depth, one)
            use_group(own_half // depth + group)

        loop(1, n1, from_first)

        def from_second(step):
            def inner(first):
                group = ((i2 + step) % n2) * n1 + first

                def one(place):
                    index = own_half + group * depth + place
                    arrive(index)
                    to_core(index)

                loop(0, depth, one)
                use_group(own_half // depth + group)

            loop(0, n1, inner)

        loop(1, n2, from_second)

        def from_core(group):
            other = (1 - core) * half
            loop(0, depth, lambda place: arrive(other + group * depth + place))
            use_group(other // depth + group)

        lax.fori_loop(0, half // depth, lambda g, c: (from_core(g), c)[1], 0)

    def finish(buffer, copies, send_sem, recv_sem):
        everything = buffer.at[pl.ds(0, copies)]
        pltpu.make_async_remote_copy(
            src_ref=everything,
            dst_ref=everything,
            send_sem=send_sem,
            recv_sem=recv_sem.at[0],
            device_id=core_peer,
            device_id_type=MESH,
        ).wait_send()

    total[...] = jnp.zeros_like(total)
    wide = depth * rows

    def first_pass(group):
        base = group * depth
        metas = [blocks[base + k, rows : rows + META, :].astype(F32) for k in range(depth)]
        meta_all = jnp.concatenate(metas, axis=1)
        policy = (meta_all[0:8] * 512.0 + meta_all[8:16]).astype(jnp.int32)
        shown = (meta_all[16:17] * 512.0 + meta_all[24:25]).astype(jnp.int32)
        squares = meta_all[25:26] + meta_all[26:27] + meta_all[27:28]
        policy_feat = rounded(features(policy))
        logged_feat[group] = rounded(features(jnp.broadcast_to(shown, (NPOL, wide))))
        others = jnp.concatenate([blocks[base + k, 0:rows, :] for k in range(depth)], axis=0)
        inner = nt_dot(own, others)
        gram = jnp.exp(inner * (2.0 / dims) - own_squares - squares).astype(BF16)
        grams[group] = gram
        total[...] += nt_dot(policy_feat, gram)

    spread(blocks, block_send, block_recv, first_pass)

    factor = NACT / (rows * count)

    def select():
        value = total[...]
        out = own_feat[0] * value[0:NPOL]
        for level in range(1, NACT):
            out += own_feat[level] * value[level * NPOL : (level + 1) * NPOL]
        return factor * out

    right_side = select()
    sides[me] = right_side
    total[...] = jnp.zeros_like(total)

    def second_pass(group):
        base = group * depth
        low = jnp.concatenate([sides[base + k] for k in range(depth)], axis=1)
        low = low.astype(BF16).astype(F32)
        feat = logged_feat[group].astype(F32)
        matched = (feat * jnp.concatenate([low] * NACT, axis=0)).astype(BF16)
        total[...] += nt_dot(matched, grams[group])

    spread(sides, side_send, side_recv, second_pass)
    image = select() + RIDGE * right_side

    lane = lax.broadcasted_iota(jnp.int32, (NPOL, rows), 1)
    sub = lax.broadcasted_iota(jnp.int32, (NPOL, rows), 0)

    def to_row(value, offset):
        column = jnp.sum(value, axis=1, keepdims=True)
        return jnp.sum(jnp.where(lane == sub + offset, column, 0.0), axis=0, keepdims=True)

    partial = (
        to_row(right_side * right_side, 0)
        + to_row(right_side * image, NPOL)
        + to_row(reward_ref[...] * right_side, 2 * NPOL)
    )

    most = max(rows_n, width)

    def all_sum(value, base, at, size, peer_of):
        slots[base + at] = value

        def copy(source, peer):
            return pltpu.make_async_remote_copy(
                src_ref=slots.at[base + source],
                dst_ref=slots.at[base + source],
                send_sem=sum_send,
                recv_sem=sum_recv.at[base + source],
                device_id=peer,
                device_id_type=MESH,
            )

        loop(1, size, lambda step: copy(at, peer_of(step)).start())
        loop(1, size, lambda step: copy((at + step) % size, core_peer).wait_recv())
        if isinstance(size, int):
            out = slots[base]
            for place in range(1, size):
                out = out + slots[base + place]
            return out
        return lax.fori_loop(
            0, size, lambda place, out: out + slots[base + place], jnp.zeros_like(value)
        )

    partial = all_sum(partial, 0, z, depth, z_peer)
    partial = all_sum(partial, depth, i1, n1, first_peer)
    partial = all_sum(partial, depth + most, i2, n2, second_peer)
    partial = all_sum(partial, depth + 2 * most, core, 2, lambda step: core_peer)

    def to_column(offset):
        spread_row = jnp.broadcast_to(partial, (NPOL, rows))
        return jnp.sum(jnp.where(lane == sub + offset, spread_row, 0.0), axis=1, keepdims=True)

    alpha = to_column(0) / to_column(NPOL)
    values_column = alpha * to_column(2 * NPOL) * (1.0 / (rows * count))
    values_ref[...] = jnp.sum(jnp.where(lane == sub, values_column, 0.0), axis=0, keepdims=True)
    square_part[0:NPOL, :] = alpha * right_side
    square_part[NPOL : 2 * NPOL, :] = right_side - alpha * image
    results = square_part[...].T
    weights_ref[...] = results[:, 0:NPOL]
    residual_ref[...] = results[:, NPOL : 2 * NPOL]

    finish(blocks, count - 1, block_send, block_recv)
    finish(sides, count - 1, side_send, side_recv)
    finish(slots, depth + rows_n + width - 2, sum_send, sum_recv)


def on_device(sizes, contexts, logged_actions, policy_actions, rewards):
    rows_n, depth, width = sizes
    rows, dims = contexts.shape
    count = 2 * rows_n * width * depth
    groups = count // depth
    most = max(rows_n, width)
    vmem = pl.BlockSpec(memory_space=pltpu.VMEM)
    weights, residual, values = pl.pallas_call(
        functools.partial(kernel, sizes),
        out_shape=(
            jax.ShapeDtypeStruct((rows, NPOL), F32),
            jax.ShapeDtypeStruct((rows, NPOL), F32),
            jax.ShapeDtypeStruct((1, rows), F32),
        ),
        in_specs=[vmem] * 4,
        out_specs=(vmem,) * 3,
        scratch_shapes=[
            pltpu.VMEM((count, rows + META, dims), BF16),
            pltpu.VMEM((count, NPOL, rows), F32),
            pltpu.VMEM((groups, rows, depth * rows), BF16),
            pltpu.VMEM((groups, NPOL * NACT, depth * rows), BF16),
            pltpu.VMEM((NPOL * NACT, rows), F32),
            pltpu.VMEM((rows, dims), F32),
            pltpu.VMEM((depth + 2 * most + 2, 1, rows), F32),
            pltpu.SemaphoreType.DMA,
            pltpu.SemaphoreType.DMA((count,)),
            pltpu.SemaphoreType.DMA,
            pltpu.SemaphoreType.DMA((count,)),
            pltpu.SemaphoreType.DMA,
            pltpu.SemaphoreType.DMA((depth + 2 * most + 2,)),
        ],
        compiler_params=pltpu.CompilerParams(
            collective_id=0, has_side_effects=True, vmem_limit_bytes=48 * 1024 * 1024
        ),
    )(contexts, logged_actions.reshape(1, rows), policy_actions, rewards.reshape(1, rows))
    return weights, residual, values[0, 0:NPOL]


def solution(mesh):
    rows_n, cols = mesh.shape["row"], mesh.shape["col"]
    depth = 4 if (cols // 2) % 4 == 0 else 1
    sizes = (rows_n, depth, cols // 2 // depth)
    placed = (
        P(("row", "col"), None),
        P(("row", "col")),
        P(("row", "col"), None),
        P(("row", "col")),
    )
    return jax.shard_map(
        functools.partial(on_device, sizes),
        mesh=mesh,
        in_specs=placed,
        out_specs=(P(("row", "col"), None), P(("row", "col"), None), P()),
        check_vma=False,
    )
```

```python
import functools
import math

import jax
import jax.numpy as jnp
from jax import lax
from jax.experimental import pallas as pl
from jax.experimental.pallas import tpu as pltpu
from jax.sharding import PartitionSpec as P

MESH = pl.DeviceIdType.MESH
F32 = jnp.float32
BF16 = jnp.bfloat16

NPOL = 8
NACT = 16
CATALOG = 131042
RIDGE = 0.1
STRIDE = 1009
PHASE = 0.37
TWO_PI = 2.0 * math.pi
META = 32


def loop(low, high, body):
    if isinstance(low, int) and isinstance(high, int) and high - low <= 4:
        for step in range(low, high):
            body(step)
    else:

        def wrapped(step, carried):
            body(step)
            return carried

        lax.fori_loop(low, high, wrapped, 0)


def cosine(turned, phase):
    whole = jnp.floor(turned.astype(F32) * (1.0 / CATALOG) + 0.5).astype(jnp.int32)
    rest = (turned - whole * CATALOG).astype(F32)
    turns = rest * (1.0 / CATALOG) + phase / TWO_PI
    turns = turns - jnp.floor(turns + 0.5)
    angle = TWO_PI * (0.25 - jnp.abs(turns))
    square = angle * angle
    series = -1.0 / 39916800.0
    for term in (362880.0, -5040.0, 120.0, -6.0, 1.0):
        series = series * square + 1.0 / term
    return series * angle


def features(chosen):
    twice = 2.0 * cosine(chosen * STRIDE, PHASE)
    before = cosine(chosen, 0.0)
    now = cosine(chosen * (1 + STRIDE), PHASE)
    scale = math.sqrt(2.0 / NACT)
    out = [jnp.full(chosen.shape, 1.0 / math.sqrt(NACT), F32)]
    for level in range(1, NACT):
        out.append(scale * now)
        before, now = now, twice * now - before
    return out


def rounded(parts):
    return jnp.concatenate(parts, axis=0).astype(BF16)


def nt_dot(left, right):
    return lax.dot_general(left, right, (((1,), (1,)), ((), ())), preferred_element_type=F32)


def kernel(
    sizes,
    ctx_ref,
    logged_ref,
    policy_ref,
    reward_ref,
    results_ref,
    blocks,
    sides,
    grams,
    logged_feat,
    total,
    logged_own,
    policy_own,
    reward_own,
    near_sums,
    plane_sums,
    load_sem,
    block_send,
    block_recv,
    side_send,
    side_recv,
    side_recv_plane,
    sum_send,
    sum_recv,
    sum_recv_plane,
):
    rows_n, depth, width = sizes
    half_groups = rows_n * width
    half = half_groups * depth
    plane = 2 * half_groups
    count = 2 * half
    rows, dims = ctx_ref.shape
    x = lax.axis_index("row")
    col = lax.axis_index("col")
    core = col % 2
    y = (col // 2) % width
    z = col // (2 * width)

    def inner_size(at_core):
        return width if rows_n == width else width + at_core * (rows_n - width)

    n1 = inner_size(core)
    n2 = inner_size(1 - core)
    i1 = y + core * (x - y)
    i2 = x + core * (y - x)
    own_half = core * half_groups
    own_group = own_half + i2 * n1 + i1
    me = own_group * depth + z

    def device(first, second, at_z, at_core):
        at_x = second + at_core * (first - second)
        at_y = first + at_core * (second - first)
        return (at_x, (at_z * width + at_y) * 2 + at_core)

    def z_peer(step):
        return device(i1, i2, (z + step) % depth, core)

    def first_peer(step):
        return device((i1 + step) % n1, i2, z, core)

    def second_peer(step):
        return device(i1, (i2 + step) % n2, z, core)

    def plane_peer(step):
        group = (own_group + step) % plane
        at_core = group // half_groups
        place = group % half_groups
        inside = inner_size(at_core)
        return device(place % inside, place // inside, z, at_core)

    core_peer = (x, (z * width + y) * 2 + 1 - core)

    barrier = pltpu.get_barrier_semaphore()

    def greet(peer):
        pl.semaphore_signal(barrier, inc=1, device_id=peer, device_id_type=MESH)

    loop(1, depth, lambda step: greet(z_peer(step)))
    loop(1, plane, lambda step: greet(plane_peer(step)))

    loads = [
        pltpu.make_async_copy(source, target, load_sem.at[place])
        for place, (source, target) in enumerate(
            (
                (ctx_ref, blocks.at[me, pl.ds(0, rows)]),
                (logged_ref, logged_own),
                (policy_ref, policy_own),
                (reward_ref, reward_own),
            )
        )
    ]
    for load in loads:
        load.start()
    for load in loads:
        load.wait()

    own = blocks[me, 0:rows, :]
    own_wide = own.astype(F32)
    own_squares = jnp.sum(own_wide * own_wide, axis=1, keepdims=True) * (1.0 / dims)
    here = lax.broadcasted_iota(jnp.int32, (rows, rows), 0)
    there = lax.broadcasted_iota(jnp.int32, (rows, rows), 1)
    squares_row = jnp.sum(jnp.where(here == there, own_squares, 0.0), axis=0, keepdims=True)

    def pieces(value):
        high = jnp.floor(value * (1.0 / 512.0) + 0.5)
        return high, value - 512.0 * high

    policy_high, policy_low = pieces(policy_own[...].astype(F32))
    logged_high, logged_low = pieces(logged_own[...].astype(F32))
    square_1 = squares_row.astype(BF16).astype(F32)
    square_2 = (squares_row - square_1).astype(BF16).astype(F32)
    square_3 = squares_row - square_1 - square_2
    meta = jnp.concatenate(
        [
            policy_high,
            policy_low,
            jnp.broadcast_to(logged_high, (8, rows)),
            logged_low,
            square_1,
            square_2,
            square_3,
            jnp.zeros((4, rows), F32),
        ],
        axis=0,
    )
    blocks[me, rows : rows + META, :] = meta.astype(BF16)
    total[...] = jnp.zeros_like(total)
    pl.semaphore_wait(barrier, (depth - 1) + (plane - 1))

    def remote(source, send_sem, recv_sem, peer):
        return pltpu.make_async_remote_copy(
            src_ref=source,
            dst_ref=source,
            send_sem=send_sem,
            recv_sem=recv_sem,
            device_id=peer,
            device_id_type=MESH,
        )

    def block_copy(index, peer):
        return remote(blocks.at[index], block_send, block_recv.at[index], peer)

    def group_copy(group):
        start = group * depth
        return remote(blocks.at[pl.ds(start, depth)], block_send, block_recv.at[start], core_peer)

    def to_first(index):
        loop(1, n1, lambda step: block_copy(index, first_peer(step)).start())

    def to_second(index):
        loop(1, n2, lambda step: block_copy(index, second_peer(step)).start())

    wide = depth * rows

    def meta_of(group):
        base = group * depth
        return jnp.concatenate(
            [blocks[base + k, rows : rows + META, :].astype(F32) for k in range(depth)], axis=1
        )

    def first_pass(group):
        base = group * depth
        meta_all = meta_of(group)
        policy = (meta_all[0:8] * 512.0 + meta_all[8:16]).astype(jnp.int32)
        squares = meta_all[25:26] + meta_all[26:27] + meta_all[27:28]
        others = jnp.concatenate([blocks[base + k, 0:rows, :] for k in range(depth)], axis=0)
        inner = nt_dot(own, others)
        policy_feat = rounded(features(policy))
        gram = jnp.exp(inner * (2.0 / dims) - own_squares - squares).astype(BF16)
        grams[group] = gram
        total[...] += nt_dot(policy_feat, gram)

    def from_core(group):
        group_copy(group).wait_recv()
        first_pass(group)

    loop(1, depth, lambda step: block_copy(me, z_peer(step)).start())
    to_first(me)
    to_second(me)

    def from_z(step):
        index = own_group * depth + (z + step) % depth
        block_copy(index, core_peer).wait_recv()
        to_first(index)
        to_second(index)

    loop(1, depth, from_z)
    group_copy(own_group).start()
    first_pass(own_group)

    def first_group(step):
        return own_half + i2 * n1 + (i1 + step) % n1

    def second_group(step, first):
        return own_half + ((i2 + step) % n2) * n1 + first

    other_half = half_groups - own_half
    peer_own = other_half + i1 * n2 + i2

    def from_first(step):
        group = first_group(step)

        def one(place):
            index = group * depth + place
            block_copy(index, core_peer).wait_recv()
            to_second(index)

        loop(0, depth, one)
        group_copy(group).start()

    loop(1, n1, from_first)
    from_core(peer_own)
    loop(1, n1, lambda step: first_pass(first_group(step)))

    def from_second(step, first):
        group = second_group(step, first)
        loop(0, depth, lambda k: block_copy(group * depth + k, core_peer).wait_recv())
        group_copy(group).start()

    loop(1, n2, lambda step: loop(0, n1, lambda first: from_second(step, first)))
    loop(1, n2, lambda step: from_core(other_half + i1 * n2 + (i2 + step) % n2))
    loop(1, n2, lambda step: loop(0, n1, lambda first: first_pass(second_group(step, first))))
    loop(
        1,
        n1,
        lambda step: loop(
            0, n2, lambda second: from_core(other_half + ((i1 + step) % n1) * n2 + second)
        ),
    )

    factor = NACT / (rows * count)
    own_feat = [
        part.astype(BF16).astype(F32)
        for part in features(jnp.broadcast_to(logged_own[...], (NPOL, rows)))
    ]

    def select():
        value = total[...]
        out = own_feat[0] * value[0:NPOL]
        for level in range(1, NACT):
            out += own_feat[level] * value[level * NPOL : (level + 1) * NPOL]
        return factor * out

    right_side = select()
    sides[me] = right_side
    total[...] = jnp.zeros_like(total)

    def side_copy(index, peer):
        return remote(sides.at[index], side_send, side_recv.at[index], peer)

    def side_group(group, peer):
        rows_of = sides.at[pl.ds(group * depth, depth)]
        return remote(rows_of, side_send, side_recv_plane.at[group], peer)

    def show(group):
        meta_all = meta_of(group)
        shown = (meta_all[16:17] * 512.0 + meta_all[24:25]).astype(jnp.int32)
        logged_feat[group] = rounded(features(jnp.broadcast_to(shown, (NPOL, wide))))

    def second_pass(group):
        base = group * depth
        low = jnp.concatenate([sides[base + k] for k in range(depth)], axis=1)
        low = low.astype(BF16).astype(F32)
        feat = logged_feat[group].astype(F32)
        matched = (feat * jnp.concatenate([low] * NACT, axis=0)).astype(BF16)
        total[...] += nt_dot(matched, grams[group])

    loop(1, depth, lambda step: side_copy(me, z_peer(step)).start())
    loop(0, half_groups, show)
    loop(1, depth, lambda k: side_copy(own_group * depth + (z + k) % depth, core_peer).wait_recv())
    loop(1, plane, lambda step: side_group(own_group, plane_peer(step)).start())
    loop(half_groups, plane, show)
    second_pass(own_group)

    def from_plane(step):
        group = (own_group + step) % plane
        side_group(group, core_peer).wait_recv()
        second_pass(group)

    loop(1, plane, from_plane)
    image = select() + RIDGE * right_side

    lane = lax.broadcasted_iota(jnp.int32, (NPOL, rows), 1)
    sub = lax.broadcasted_iota(jnp.int32, (NPOL, rows), 0)

    def to_row(value, offset):
        column = jnp.sum(value, axis=1, keepdims=True)
        return jnp.sum(jnp.where(lane == sub + offset, column, 0.0), axis=0, keepdims=True)

    partial = (
        to_row(right_side * right_side, 0)
        + to_row(right_side * image, NPOL)
        + to_row(reward_own[...] * right_side, 2 * NPOL)
    )

    def all_sum(value, slots, recv, at, size, peer_of):
        slots[at] = value
        loop(
            1,
            size,
            lambda step: remote(slots.at[at], sum_send, recv.at[at], peer_of(step)).start(),
        )

        def arrive(step):
            place = (at + step) % size
            remote(slots.at[place], sum_send, recv.at[place], core_peer).wait_recv()

        loop(1, size, arrive)
        return jnp.sum(slots[...], axis=0)

    partial = all_sum(partial, near_sums, sum_recv, z, depth, z_peer)
    partial = all_sum(partial, plane_sums, sum_recv_plane, own_group, plane, plane_peer)

    def to_column(offset):
        spread_row = jnp.broadcast_to(partial, (NPOL, rows))
        return jnp.sum(jnp.where(lane == sub + offset, spread_row, 0.0), axis=1, keepdims=True)

    alpha = to_column(0) / to_column(NPOL)
    values_column = alpha * to_column(2 * NPOL) * (1.0 / (rows * count))
    values_row = jnp.sum(jnp.where(lane == sub, values_column, 0.0), axis=0, keepdims=True)
    results_ref[0:NPOL] = alpha * right_side
    results_ref[NPOL : 2 * NPOL] = right_side - alpha * image
    results_ref[2 * NPOL :] = jnp.broadcast_to(values_row, (NPOL, rows))

    remote(
        blocks.at[pl.ds(0, count - 1)], block_send, block_recv.at[0], core_peer
    ).wait_send()
    remote(sides.at[pl.ds(0, count - 1)], side_send, side_recv.at[0], core_peer).wait_send()
    remote(
        near_sums.at[pl.ds(0, depth - 1)], sum_send, sum_recv.at[0], core_peer
    ).wait_send()
    remote(
        plane_sums.at[pl.ds(0, plane - 1)], sum_send, sum_recv_plane.at[0], core_peer
    ).wait_send()


def on_device(sizes, contexts, logged_actions, policy_actions, rewards):
    rows_n, depth, width = sizes
    rows, dims = contexts.shape
    plane = 2 * rows_n * width
    count = plane * depth
    vmem = pl.BlockSpec(memory_space=pltpu.VMEM)
    hbm = pl.BlockSpec(memory_space=pltpu.HBM)
    results = pl.pallas_call(
        functools.partial(kernel, sizes),
        out_shape=jax.ShapeDtypeStruct((3 * NPOL, rows), F32),
        in_specs=[hbm] * 4,
        out_specs=vmem,
        scratch_shapes=[
            pltpu.VMEM((count, rows + META, dims), BF16),
            pltpu.VMEM((count, NPOL, rows), F32),
            pltpu.VMEM((plane, rows, depth * rows), BF16),
            pltpu.VMEM((plane, NPOL * NACT, depth * rows), BF16),
            pltpu.VMEM((NPOL * NACT, rows), F32),
            pltpu.VMEM((1, rows), jnp.int32),
            pltpu.VMEM((NPOL, rows), jnp.int32),
            pltpu.VMEM((1, rows), F32),
            pltpu.VMEM((depth, 1, rows), F32),
            pltpu.VMEM((plane, 1, rows), F32),
            pltpu.SemaphoreType.DMA((4,)),
            pltpu.SemaphoreType.DMA,
            pltpu.SemaphoreType.DMA((count,)),
            pltpu.SemaphoreType.DMA,
            pltpu.SemaphoreType.DMA((count,)),
            pltpu.SemaphoreType.DMA((plane,)),
            pltpu.SemaphoreType.DMA,
            pltpu.SemaphoreType.DMA((depth,)),
            pltpu.SemaphoreType.DMA((plane,)),
        ],
        compiler_params=pltpu.CompilerParams(
            collective_id=0, has_side_effects=True, vmem_limit_bytes=60 * 1024 * 1024
        ),
    )(contexts, logged_actions.reshape(1, rows), policy_actions.T, rewards.reshape(1, rows))
    return results[0:NPOL].T, results[NPOL : 2 * NPOL].T, results[2 * NPOL, 0:NPOL]


def solution(mesh):
    rows_n, cols = mesh.shape["row"], mesh.shape["col"]
    depth = 4 if (cols // 2) % 4 == 0 else 1
    sizes = (rows_n, depth, cols // 2 // depth)
    placed = (
        P(("row", "col"), None),
        P(("row", "col")),
        P(("row", "col"), None),
        P(("row", "col")),
    )
    return jax.shard_map(
        functools.partial(on_device, sizes),
        mesh=mesh,
        in_specs=placed,
        out_specs=(P(("row", "col"), None), P(("row", "col"), None), P()),
        check_vma=False,
    )
```

```python
import functools
import math

import jax
import jax.numpy as jnp
from jax import lax
from jax.experimental import pallas as pl
from jax.experimental.pallas import tpu as pltpu
from jax.sharding import PartitionSpec as P

MESH = pl.DeviceIdType.MESH
F32 = jnp.float32
BF16 = jnp.bfloat16

NPOL = 8
NACT = 16
CATALOG = 131042
RIDGE = 0.1
STRIDE = 1009
PHASE = 0.37
TWO_PI = 2.0 * math.pi
META = 32


def loop(low, high, body):
    if isinstance(low, int) and isinstance(high, int) and high - low <= 4:
        for step in range(low, high):
            body(step)
    else:

        def wrapped(step, carried):
            body(step)
            return carried

        lax.fori_loop(low, high, wrapped, 0)


def cosine(turned, phase):
    whole = jnp.floor(turned.astype(F32) * (1.0 / CATALOG) + 0.5).astype(jnp.int32)
    rest = (turned - whole * CATALOG).astype(F32)
    turns = rest * (1.0 / CATALOG) + phase / TWO_PI
    turns = turns - jnp.floor(turns + 0.5)
    angle = TWO_PI * (0.25 - jnp.abs(turns))
    square = angle * angle
    series = -1.0 / 39916800.0
    for term in (362880.0, -5040.0, 120.0, -6.0, 1.0):
        series = series * square + 1.0 / term
    return series * angle


def features(chosen):
    twice = 2.0 * cosine(chosen * STRIDE, PHASE)
    before = cosine(chosen, 0.0)
    now = cosine(chosen * (1 + STRIDE), PHASE)
    scale = math.sqrt(2.0 / NACT)
    out = [jnp.full(chosen.shape, 1.0 / math.sqrt(NACT), F32)]
    for level in range(1, NACT):
        out.append(scale * now)
        before, now = now, twice * now - before
    return out


def rounded(parts):
    return jnp.concatenate(parts, axis=0).astype(BF16)


def nt_dot(left, right):
    return lax.dot_general(left, right, (((1,), (1,)), ((), ())), preferred_element_type=F32)


def kernel(
    sizes,
    ctx_ref,
    logged_ref,
    policy_ref,
    reward_ref,
    results_ref,
    blocks,
    near,
    sides,
    grams,
    logged_feat,
    total,
    logged_own,
    policy_own,
    reward_own,
    near_sums,
    plane_sums,
    load_sem,
    block_send,
    block_recv,
    near_send,
    near_recv,
    side_send,
    side_recv,
    sum_send,
    sum_recv,
    sum_recv_plane,
):
    rows_n, depth, width = sizes
    half_groups = rows_n * width
    half = half_groups * depth
    plane = 2 * half_groups
    count = 2 * half
    rows, dims = ctx_ref.shape
    x = lax.axis_index("row")
    col = lax.axis_index("col")
    core = lax.rem(col, 2)
    y = lax.rem(lax.div(col, 2), width)
    z = lax.div(col, 2 * width)

    def inner_size(at_core):
        return width if rows_n == width else width + at_core * (rows_n - width)

    n1 = inner_size(core)
    n2 = inner_size(1 - core)
    i1 = y + core * (x - y)
    i2 = x + core * (y - x)
    own_half = core * half_groups
    own_group = own_half + i2 * n1 + i1
    me = own_group * depth + z

    def device(first, second, at_z, at_core):
        at_x = second + at_core * (first - second)
        at_y = first + at_core * (second - first)
        return (at_x, (at_z * width + at_y) * 2 + at_core)

    def z_peer(step):
        return device(i1, i2, lax.rem(z + step, depth), core)

    def first_peer(step):
        return device(lax.rem(i1 + step, n1), i2, z, core)

    def second_peer(step):
        return device(i1, lax.rem(i2 + step, n2), z, core)

    def plane_peer(step):
        group = lax.rem(own_group + step, plane)
        at_core = lax.div(group, half_groups)
        place = lax.rem(group, half_groups)
        inside = inner_size(at_core)
        return device(lax.rem(place, inside), lax.div(place, inside), z, at_core)

    core_peer = (x, (z * width + y) * 2 + 1 - core)

    barrier = pltpu.get_barrier_semaphore()

    def greet(peer):
        pl.semaphore_signal(barrier, inc=1, device_id=peer, device_id_type=MESH)

    loop(1, depth, lambda step: greet(z_peer(step)))
    loop(1, plane, lambda step: greet(plane_peer(step)))

    loads = [
        pltpu.make_async_copy(source, target, load_sem.at[place])
        for place, (source, target) in enumerate(
            (
                (ctx_ref, blocks.at[me, pl.ds(0, rows)]),
                (logged_ref, logged_own),
                (policy_ref, policy_own),
                (reward_ref, reward_own),
            )
        )
    ]
    for load in loads:
        load.start()
    for load in loads:
        load.wait()

    own = blocks[me, 0:rows, :]
    own_wide = own.astype(F32)
    own_squares = jnp.sum(own_wide * own_wide, axis=1, keepdims=True) * (1.0 / dims)
    here = lax.broadcasted_iota(jnp.int32, (rows, rows), 0)
    there = lax.broadcasted_iota(jnp.int32, (rows, rows), 1)
    squares_row = jnp.sum(jnp.where(here == there, own_squares, 0.0), axis=0, keepdims=True)

    def pieces(value):
        high = jnp.floor(value * (1.0 / 512.0) + 0.5)
        return high, value - 512.0 * high

    policy_high, policy_low = pieces(policy_own[...].astype(F32))
    logged_high, logged_low = pieces(logged_own[...].astype(F32))
    square_1 = squares_row.astype(BF16).astype(F32)
    square_2 = (squares_row - square_1).astype(BF16).astype(F32)
    square_3 = squares_row - square_1 - square_2
    meta = jnp.concatenate(
        [
            policy_high,
            policy_low,
            jnp.broadcast_to(logged_high, (8, rows)),
            logged_low,
            square_1,
            square_2,
            square_3,
            jnp.zeros((4, rows), F32),
        ],
        axis=0,
    )
    blocks[me, rows : rows + META, :] = meta.astype(BF16)
    total[...] = jnp.zeros_like(total)
    pl.semaphore_wait(barrier, (depth - 1) + (plane - 1))

    def remote(source, send_sem, recv_sem, peer):
        return pltpu.make_async_remote_copy(
            src_ref=source,
            dst_ref=source,
            send_sem=send_sem,
            recv_sem=recv_sem,
            device_id=peer,
            device_id_type=MESH,
        )

    def block_copy(index, peer):
        return remote(blocks.at[index], block_send, block_recv.at[index], peer)

    def group_copy(group):
        start = group * depth
        return remote(blocks.at[pl.ds(start, depth)], block_send, block_recv.at[start], core_peer)

    def to_first(index):
        loop(1, n1, lambda step: block_copy(index, first_peer(step)).start())

    def to_second(index):
        loop(1, n2, lambda step: block_copy(index, second_peer(step)).start())

    wide = depth * rows

    def meta_of(group):
        base = group * depth
        return jnp.concatenate(
            [blocks[base + k, rows : rows + META, :].astype(F32) for k in range(depth)], axis=1
        )

    def first_pass(group):
        base = group * depth
        meta_all = meta_of(group)
        policy = (meta_all[0:8] * 512.0 + meta_all[8:16]).astype(jnp.int32)
        squares = meta_all[25:26] + meta_all[26:27] + meta_all[27:28]
        others = jnp.concatenate([blocks[base + k, 0:rows, :] for k in range(depth)], axis=0)
        inner = nt_dot(own, others)
        policy_feat = rounded(features(policy))
        gram = jnp.exp(inner * (2.0 / dims) - own_squares - squares).astype(BF16)
        grams[group] = gram
        total[...] += nt_dot(policy_feat, gram)

    def from_core(group):
        group_copy(group).wait_recv()
        first_pass(group)

    loop(1, depth, lambda step: block_copy(me, z_peer(step)).start())
    to_first(me)
    to_second(me)

    def from_z(step):
        index = own_group * depth + lax.rem(z + step, depth)
        block_copy(index, core_peer).wait_recv()
        to_first(index)
        to_second(index)

    loop(1, depth, from_z)
    group_copy(own_group).start()
    first_pass(own_group)

    def first_group(step):
        return own_half + i2 * n1 + lax.rem(i1 + step, n1)

    def second_group(place):
        step = 1 + lax.div(place, n1)
        first = lax.rem(i1 + lax.rem(place, n1), n1)
        return own_half + lax.rem(i2 + step, n2) * n1 + first

    other_half = half_groups - own_half
    peer_own = other_half + i1 * n2 + i2

    def from_first(step):
        group = first_group(step)

        def one(place):
            index = group * depth + place
            block_copy(index, core_peer).wait_recv()
            to_second(index)

        loop(0, depth, one)
        group_copy(group).start()

    def peer_first(step):
        return other_half + i1 * n2 + lax.rem(i2 + step, n2)

    def peer_second(place):
        step = 1 + lax.div(place, n2)
        second = lax.rem(i2 + lax.rem(place, n2), n2)
        return other_half + lax.rem(i1 + step, n1) * n2 + second

    def from_second(place):
        group = second_group(place)
        loop(0, depth, lambda k: block_copy(group * depth + k, core_peer).wait_recv())
        group_copy(group).start()

    own_last = (n2 - 1) * n1
    peer_last = (n1 - 1) * n2
    loop(1, n1, from_first)
    from_core(peer_own)
    loop(1, n1, lambda step: first_pass(first_group(step)))
    if rows_n == width:
        for place in range(own_last):
            from_second(place)
            if place == 0:
                loop(1, n2, lambda step: from_core(peer_first(step)))
            else:
                from_core(peer_second(place - 1))
            first_pass(second_group(place))
        from_core(peer_second(own_last - 1))
    else:
        loop(0, own_last, from_second)
        loop(1, n2, lambda step: from_core(peer_first(step)))
        loop(0, own_last, lambda place: first_pass(second_group(place)))
        loop(0, peer_last, lambda place: from_core(peer_second(place)))

    factor = NACT / (rows * count)
    own_feat = [
        part.astype(BF16).astype(F32)
        for part in features(jnp.broadcast_to(logged_own[...], (NPOL, rows)))
    ]

    def select():
        value = total[...]
        out = own_feat[0] * value[0:NPOL]
        for level in range(1, NACT):
            out += own_feat[level] * value[level * NPOL : (level + 1) * NPOL]
        return factor * out

    right_side = select()
    near[z] = right_side
    total[...] = jnp.zeros_like(total)

    def near_copy(place, peer):
        return remote(near.at[place], near_send, near_recv.at[place], peer)

    def side_copy(group, peer):
        return remote(sides.at[group], side_send, side_recv.at[group], peer)

    def show(group):
        meta_all = meta_of(group)
        shown = (meta_all[16:17] * 512.0 + meta_all[24:25]).astype(jnp.int32)
        logged_feat[group] = rounded(features(jnp.broadcast_to(shown, (NPOL, wide))))

    def second_pass(group):
        packed = sides[group].astype(F32)
        low = jnp.concatenate([packed[k * NPOL : (k + 1) * NPOL] for k in range(depth)], axis=1)
        feat = logged_feat[group].astype(F32)
        matched = (feat * jnp.concatenate([low] * NACT, axis=0)).astype(BF16)
        total[...] += nt_dot(matched, grams[group])

    loop(1, depth, lambda step: near_copy(z, z_peer(step)).start())
    loop(0, half_groups, show)
    loop(1, depth, lambda step: near_copy(lax.rem(z + step, depth), core_peer).wait_recv())
    sides[own_group] = rounded([near[k] for k in range(depth)])
    loop(1, plane, lambda step: side_copy(own_group, plane_peer(step)).start())
    loop(half_groups, plane, show)
    second_pass(own_group)

    def from_plane(step):
        group = lax.rem(own_group + step, plane)
        side_copy(group, core_peer).wait_recv()
        second_pass(group)

    loop(1, plane, from_plane)
    image = select() + RIDGE * right_side

    lane = lax.broadcasted_iota(jnp.int32, (NPOL, rows), 1)
    sub = lax.broadcasted_iota(jnp.int32, (NPOL, rows), 0)

    def to_row(value, offset):
        column = jnp.sum(value, axis=1, keepdims=True)
        return jnp.sum(jnp.where(lane == sub + offset, column, 0.0), axis=0, keepdims=True)

    partial = (
        to_row(right_side * right_side, 0)
        + to_row(right_side * image, NPOL)
        + to_row(reward_own[...] * right_side, 2 * NPOL)
    )

    def all_sum(value, slots, recv, at, size, peer_of):
        slots[at] = value
        loop(
            1,
            size,
            lambda step: remote(slots.at[at], sum_send, recv.at[at], peer_of(step)).start(),
        )

        def arrive(step):
            place = lax.rem(at + step, size)
            remote(slots.at[place], sum_send, recv.at[place], core_peer).wait_recv()

        loop(1, size, arrive)
        return jnp.sum(slots[...], axis=0)

    partial = all_sum(partial, near_sums, sum_recv, z, depth, z_peer)
    partial = all_sum(partial, plane_sums, sum_recv_plane, own_group, plane, plane_peer)

    def to_column(offset):
        spread_row = jnp.broadcast_to(partial, (NPOL, rows))
        return jnp.sum(jnp.where(lane == sub + offset, spread_row, 0.0), axis=1, keepdims=True)

    alpha = to_column(0) / to_column(NPOL)
    values_column = alpha * to_column(2 * NPOL) * (1.0 / (rows * count))
    values_row = jnp.sum(jnp.where(lane == sub, values_column, 0.0), axis=0, keepdims=True)
    results_ref[0:NPOL] = alpha * right_side
    results_ref[NPOL : 2 * NPOL] = right_side - alpha * image
    results_ref[2 * NPOL :] = jnp.broadcast_to(values_row, (NPOL, rows))

    remote(
        blocks.at[pl.ds(0, count - 1)], block_send, block_recv.at[0], core_peer
    ).wait_send()
    remote(near.at[pl.ds(0, depth - 1)], near_send, near_recv.at[0], core_peer).wait_send()
    remote(sides.at[pl.ds(0, plane - 1)], side_send, side_recv.at[0], core_peer).wait_send()
    remote(
        near_sums.at[pl.ds(0, depth - 1)], sum_send, sum_recv.at[0], core_peer
    ).wait_send()
    remote(
        plane_sums.at[pl.ds(0, plane - 1)], sum_send, sum_recv_plane.at[0], core_peer
    ).wait_send()


def on_device(sizes, contexts, logged_actions, policy_actions, rewards):
    rows_n, depth, width = sizes
    rows, dims = contexts.shape
    plane = 2 * rows_n * width
    count = plane * depth
    vmem = pl.BlockSpec(memory_space=pltpu.VMEM)
    hbm = pl.BlockSpec(memory_space=pltpu.HBM)
    results = pl.pallas_call(
        functools.partial(kernel, sizes),
        out_shape=jax.ShapeDtypeStruct((3 * NPOL, rows), F32),
        in_specs=[hbm] * 4,
        out_specs=vmem,
        scratch_shapes=[
            pltpu.VMEM((count, rows + META, dims), BF16),
            pltpu.VMEM((depth, NPOL, rows), F32),
            pltpu.VMEM((plane, depth * NPOL, rows), BF16),
            pltpu.VMEM((plane, rows, depth * rows), BF16),
            pltpu.VMEM((plane, NPOL * NACT, depth * rows), BF16),
            pltpu.VMEM((NPOL * NACT, rows), F32),
            pltpu.VMEM((1, rows), jnp.int32),
            pltpu.VMEM((NPOL, rows), jnp.int32),
            pltpu.VMEM((1, rows), F32),
            pltpu.VMEM((depth, 1, rows), F32),
            pltpu.VMEM((plane, 1, rows), F32),
            pltpu.SemaphoreType.DMA((4,)),
            pltpu.SemaphoreType.DMA,
            pltpu.SemaphoreType.DMA((count,)),
            pltpu.SemaphoreType.DMA,
            pltpu.SemaphoreType.DMA((depth,)),
            pltpu.SemaphoreType.DMA,
            pltpu.SemaphoreType.DMA((plane,)),
            pltpu.SemaphoreType.DMA,
            pltpu.SemaphoreType.DMA((depth,)),
            pltpu.SemaphoreType.DMA((plane,)),
        ],
        compiler_params=pltpu.CompilerParams(
            collective_id=0, has_side_effects=True, vmem_limit_bytes=48 * 1024 * 1024
        ),
    )(contexts, logged_actions.reshape(1, rows), policy_actions.T, rewards.reshape(1, rows))
    return results[0:NPOL].T, results[NPOL : 2 * NPOL].T, results[2 * NPOL, 0:NPOL]


def solution(mesh):
    rows_n, cols = mesh.shape["row"], mesh.shape["col"]
    depth = 4 if (cols // 2) % 4 == 0 else 1
    sizes = (rows_n, depth, cols // 2 // depth)
    placed = (
        P(("row", "col"), None),
        P(("row", "col")),
        P(("row", "col"), None),
        P(("row", "col")),
    )
    return jax.shard_map(
        functools.partial(on_device, sizes),
        mesh=mesh,
        in_specs=placed,
        out_specs=(P(("row", "col"), None), P(("row", "col"), None), P()),
        check_vma=False,
    )
```

```python
import functools
import math

import jax
import jax.numpy as jnp
from jax import lax
from jax.experimental import pallas as pl
from jax.experimental.pallas import tpu as pltpu
from jax.sharding import PartitionSpec as P

MESH = pl.DeviceIdType.MESH
F32 = jnp.float32
BF16 = jnp.bfloat16

NPOL = 8
NACT = 16
CATALOG = 131042
RIDGE = 0.1
STRIDE = 1009
PHASE = 0.37
TWO_PI = 2.0 * math.pi
META = 32


def loop(low, high, body):
    if isinstance(low, int) and isinstance(high, int) and high - low <= 4:
        for step in range(low, high):
            body(step)
    else:

        def wrapped(step, carried):
            body(step)
            return carried

        lax.fori_loop(low, high, wrapped, 0)


def cosine(turned, phase):
    whole = jnp.floor(turned.astype(F32) * (1.0 / CATALOG) + 0.5).astype(jnp.int32)
    rest = (turned - whole * CATALOG).astype(F32)
    turns = rest * (1.0 / CATALOG) + phase / TWO_PI
    turns = turns - jnp.floor(turns + 0.5)
    angle = TWO_PI * (0.25 - jnp.abs(turns))
    square = angle * angle
    series = -1.0 / 39916800.0
    for term in (362880.0, -5040.0, 120.0, -6.0, 1.0):
        series = series * square + 1.0 / term
    return series * angle


def features(chosen):
    twice = 2.0 * cosine(chosen * STRIDE, PHASE)
    before = cosine(chosen, 0.0)
    now = cosine(chosen * (1 + STRIDE), PHASE)
    scale = math.sqrt(2.0 / NACT)
    out = [jnp.full(chosen.shape, 1.0 / math.sqrt(NACT), F32)]
    for level in range(1, NACT):
        out.append(scale * now)
        before, now = now, twice * now - before
    return out


def rounded(parts):
    return jnp.concatenate(parts, axis=0).astype(BF16)


def dot(left, right, over=1):
    return lax.dot_general(left, right, (((over,), (0,)), ((), ())), preferred_element_type=F32)


def kernel(
    sizes,
    ctx_ref,
    logged_ref,
    policy_ref,
    reward_ref,
    results_ref,
    blocks,
    near,
    sides,
    grams,
    logged_feat,
    total,
    near_sums,
    plane_sums,
    block_send,
    block_recv,
    near_send,
    near_recv,
    side_send,
    side_recv,
    sum_send,
    sum_recv,
    sum_recv_plane,
):
    rows_n, depth, width = sizes
    half_groups = rows_n * width
    half = half_groups * depth
    plane = 2 * half_groups
    count = 2 * half
    rows, dims = ctx_ref.shape
    x = lax.axis_index("row")
    col = lax.axis_index("col")
    core = lax.rem(col, 2)
    y = lax.rem(lax.div(col, 2), width)
    z = lax.div(col, 2 * width)

    def inner_size(at_core):
        return width if rows_n == width else width + at_core * (rows_n - width)

    n1 = inner_size(core)
    n2 = inner_size(1 - core)
    i1 = y + core * (x - y)
    i2 = x + core * (y - x)
    own_half = core * half_groups
    own_group = own_half + i2 * n1 + i1
    me = own_group * depth + z

    def device(first, second, at_z, at_core):
        at_x = second + at_core * (first - second)
        at_y = first + at_core * (second - first)
        return (at_x, (at_z * width + at_y) * 2 + at_core)

    def z_peer(step):
        return device(i1, i2, lax.rem(z + step, depth), core)

    def first_peer(step):
        return device(lax.rem(i1 + step, n1), i2, z, core)

    def second_peer(step):
        return device(i1, lax.rem(i2 + step, n2), z, core)

    def plane_peer(step):
        group = lax.rem(own_group + step, plane)
        at_core = lax.div(group, half_groups)
        place = lax.rem(group, half_groups)
        inside = inner_size(at_core)
        return device(lax.rem(place, inside), lax.div(place, inside), z, at_core)

    core_peer = (x, (z * width + y) * 2 + 1 - core)

    barrier = pltpu.get_barrier_semaphore()

    def greet(peer):
        pl.semaphore_signal(barrier, inc=1, device_id=peer, device_id_type=MESH)

    loop(1, depth, lambda step: greet(z_peer(step)))
    loop(1, plane, lambda step: greet(plane_peer(step)))

    own = ctx_ref[...]
    blocks[me, 0:rows, :] = own
    own_wide = own.astype(F32)
    own_squares = jnp.sum(own_wide * own_wide, axis=1, keepdims=True) * (1.0 / dims)
    here = lax.broadcasted_iota(jnp.int32, (rows, rows), 0)
    there = lax.broadcasted_iota(jnp.int32, (rows, rows), 1)
    squares_row = jnp.sum(jnp.where(here == there, own_squares, 0.0), axis=0, keepdims=True)
    own_turned = own_wide.T.astype(BF16)
    place = lax.broadcasted_iota(jnp.int32, (META // 2, rows), 0)
    picks = jnp.where((place >= 9) & (place <= 11), -0.5 * dims, 0.0).astype(BF16)

    def pieces(value):
        high = jnp.floor(value * (1.0 / 512.0) + 0.5)
        return high, value - 512.0 * high

    policy_high, policy_low = pieces(policy_ref[...].astype(F32))
    logged_high, logged_low = pieces(logged_ref[...].astype(F32))
    square_1 = squares_row.astype(BF16).astype(F32)
    square_2 = (squares_row - square_1).astype(BF16).astype(F32)
    square_3 = squares_row - square_1 - square_2
    meta = jnp.concatenate(
        [
            policy_high,
            policy_low,
            jnp.broadcast_to(logged_high, (8, rows)),
            logged_low,
            square_1,
            square_2,
            square_3,
            jnp.zeros((4, rows), F32),
        ],
        axis=0,
    )
    blocks[me, rows : rows + META, :] = meta.astype(BF16)
    total[...] = jnp.zeros_like(total)
    pl.semaphore_wait(barrier, (depth - 1) + (plane - 1))

    def remote(source, send_sem, recv_sem, peer):
        return pltpu.make_async_remote_copy(
            src_ref=source,
            dst_ref=source,
            send_sem=send_sem,
            recv_sem=recv_sem,
            device_id=peer,
            device_id_type=MESH,
        )

    def block_copy(index, peer):
        return remote(blocks.at[index], block_send, block_recv.at[index], peer)

    def group_copy(group):
        start = group * depth
        return remote(blocks.at[pl.ds(start, depth)], block_send, block_recv.at[start], core_peer)

    def to_first(index):
        loop(1, n1, lambda step: block_copy(index, first_peer(step)).start())

    def to_second(index):
        loop(1, n2, lambda step: block_copy(index, second_peer(step)).start())

    wide = depth * rows

    def meta_of(group):
        base = group * depth
        return jnp.concatenate(
            [blocks[base + k, rows : rows + META, :].astype(F32) for k in range(depth)], axis=1
        )

    def first_pass(group):
        base = group * depth
        meta_all = meta_of(group)
        policy = (meta_all[0:8] * 512.0 + meta_all[8:16]).astype(jnp.int32)
        others = jnp.concatenate([blocks[base + k, 0:rows, :] for k in range(depth)], axis=0)
        squares = jnp.concatenate(
            [blocks[base + k, rows + META // 2 : rows + META, :] for k in range(depth)], axis=1
        )
        inner = dot(others, own_turned) + dot(squares, picks, 0)
        policy_feat = rounded(features(policy))
        gram = jnp.exp(inner * (2.0 / dims) - squares_row).astype(BF16)
        grams[group] = gram
        total[...] += dot(policy_feat, gram)

    def from_core(group):
        group_copy(group).wait_recv()
        first_pass(group)

    loop(1, depth, lambda step: block_copy(me, z_peer(step)).start())
    to_first(me)
    to_second(me)

    def from_z(step):
        index = own_group * depth + lax.rem(z + step, depth)
        block_copy(index, core_peer).wait_recv()
        to_first(index)
        to_second(index)

    loop(1, depth, from_z)
    group_copy(own_group).start()
    first_pass(own_group)

    def first_group(step):
        return own_half + i2 * n1 + lax.rem(i1 + step, n1)

    def second_group(place):
        step = 1 + lax.div(place, n1)
        first = lax.rem(i1 + lax.rem(place, n1), n1)
        return own_half + lax.rem(i2 + step, n2) * n1 + first

    other_half = half_groups - own_half
    peer_own = other_half + i1 * n2 + i2

    def from_first(step):
        group = first_group(step)

        def one(place):
            index = group * depth + place
            block_copy(index, core_peer).wait_recv()
            to_second(index)

        loop(0, depth, one)
        group_copy(group).start()

    def peer_first(step):
        return other_half + i1 * n2 + lax.rem(i2 + step, n2)

    def peer_second(place):
        step = 1 + lax.div(place, n2)
        second = lax.rem(i2 + lax.rem(place, n2), n2)
        return other_half + lax.rem(i1 + step, n1) * n2 + second

    def from_second(place):
        group = second_group(place)
        loop(0, depth, lambda k: block_copy(group * depth + k, core_peer).wait_recv())
        group_copy(group).start()

    own_last = (n2 - 1) * n1
    peer_last = (n1 - 1) * n2
    loop(1, n1, from_first)
    from_core(peer_own)
    loop(1, n1, lambda step: first_pass(first_group(step)))
    if rows_n == width:
        for place in range(own_last):
            from_second(place)
            if place == 0:
                loop(1, n2, lambda step: from_core(peer_first(step)))
            else:
                from_core(peer_second(place - 1))
            first_pass(second_group(place))
        from_core(peer_second(own_last - 1))
    else:
        loop(0, own_last, from_second)
        loop(1, n2, lambda step: from_core(peer_first(step)))
        loop(0, own_last, lambda place: first_pass(second_group(place)))
        loop(0, peer_last, lambda place: from_core(peer_second(place)))

    factor = NACT / (rows * count)
    own_feat = [
        part.astype(BF16).astype(F32)
        for part in features(jnp.broadcast_to(logged_ref[...], (NPOL, rows)))
    ]

    def select():
        value = total[...]
        out = own_feat[0] * value[0:NPOL]
        for level in range(1, NACT):
            out += own_feat[level] * value[level * NPOL : (level + 1) * NPOL]
        return factor * out

    right_side = select()
    near[z] = right_side
    total[...] = jnp.zeros_like(total)

    def near_copy(place, peer):
        return remote(near.at[place], near_send, near_recv.at[place], peer)

    def side_copy(group, peer):
        return remote(sides.at[group], side_send, side_recv.at[group], peer)

    def show(group):
        meta_all = meta_of(group)
        shown = (meta_all[16:17] * 512.0 + meta_all[24:25]).astype(jnp.int32)
        logged_feat[group] = rounded(features(jnp.broadcast_to(shown, (NPOL, wide))))

    def second_pass(group):
        packed = sides[group].astype(F32)
        low = jnp.concatenate([packed[k * NPOL : (k + 1) * NPOL] for k in range(depth)], axis=1)
        feat = logged_feat[group].astype(F32)
        matched = (feat * jnp.concatenate([low] * NACT, axis=0)).astype(BF16)
        total[...] += dot(matched, grams[group])

    loop(1, depth, lambda step: near_copy(z, z_peer(step)).start())
    loop(0, half_groups, show)
    loop(1, depth, lambda step: near_copy(lax.rem(z + step, depth), core_peer).wait_recv())
    sides[own_group] = rounded([near[k] for k in range(depth)])
    loop(1, plane, lambda step: side_copy(own_group, plane_peer(step)).start())
    loop(half_groups, plane, show)
    second_pass(own_group)

    def from_plane(step):
        group = lax.rem(own_group + step, plane)
        side_copy(group, core_peer).wait_recv()
        second_pass(group)

    loop(1, plane, from_plane)
    image = select() + RIDGE * right_side

    lane = lax.broadcasted_iota(jnp.int32, (NPOL, rows), 1)
    sub = lax.broadcasted_iota(jnp.int32, (NPOL, rows), 0)

    def to_row(value, offset):
        column = jnp.sum(value, axis=1, keepdims=True)
        return jnp.sum(jnp.where(lane == sub + offset, column, 0.0), axis=0, keepdims=True)

    partial = (
        to_row(right_side * right_side, 0)
        + to_row(right_side * image, NPOL)
        + to_row(reward_ref[...] * right_side, 2 * NPOL)
    )

    def all_sum(value, slots, recv, at, size, peer_of):
        slots[at] = value
        loop(
            1,
            size,
            lambda step: remote(slots.at[at], sum_send, recv.at[at], peer_of(step)).start(),
        )

        def arrive(step):
            place = lax.rem(at + step, size)
            remote(slots.at[place], sum_send, recv.at[place], core_peer).wait_recv()

        loop(1, size, arrive)
        return jnp.sum(slots[...], axis=0)

    partial = all_sum(partial, near_sums, sum_recv, z, depth, z_peer)
    partial = all_sum(partial, plane_sums, sum_recv_plane, own_group, plane, plane_peer)

    def to_column(offset):
        spread_row = jnp.broadcast_to(partial, (NPOL, rows))
        return jnp.sum(jnp.where(lane == sub + offset, spread_row, 0.0), axis=1, keepdims=True)

    alpha = to_column(0) / to_column(NPOL)
    values_column = alpha * to_column(2 * NPOL) * (1.0 / (rows * count))
    values_row = jnp.sum(jnp.where(lane == sub, values_column, 0.0), axis=0, keepdims=True)
    results_ref[0:NPOL] = alpha * right_side
    results_ref[NPOL : 2 * NPOL] = right_side - alpha * image
    results_ref[2 * NPOL :] = jnp.broadcast_to(values_row, (NPOL, rows))

    remote(
        blocks.at[pl.ds(0, count - 1)], block_send, block_recv.at[0], core_peer
    ).wait_send()
    remote(near.at[pl.ds(0, depth - 1)], near_send, near_recv.at[0], core_peer).wait_send()
    remote(sides.at[pl.ds(0, plane - 1)], side_send, side_recv.at[0], core_peer).wait_send()
    remote(
        near_sums.at[pl.ds(0, depth - 1)], sum_send, sum_recv.at[0], core_peer
    ).wait_send()
    remote(
        plane_sums.at[pl.ds(0, plane - 1)], sum_send, sum_recv_plane.at[0], core_peer
    ).wait_send()


def on_device(sizes, contexts, logged_actions, policy_actions, rewards):
    rows_n, depth, width = sizes
    rows, dims = contexts.shape
    plane = 2 * rows_n * width
    count = plane * depth
    vmem = pl.BlockSpec(memory_space=pltpu.VMEM)
    results = pl.pallas_call(
        functools.partial(kernel, sizes),
        out_shape=jax.ShapeDtypeStruct((3 * NPOL, rows), F32),
        in_specs=[vmem] * 4,
        out_specs=vmem,
        scratch_shapes=[
            pltpu.VMEM((count, rows + META, dims), BF16),
            pltpu.VMEM((depth, NPOL, rows), F32),
            pltpu.VMEM((plane, depth * NPOL, rows), BF16),
            pltpu.VMEM((plane, depth * rows, rows), BF16),
            pltpu.VMEM((plane, NPOL * NACT, depth * rows), BF16),
            pltpu.VMEM((NPOL * NACT, rows), F32),
            pltpu.VMEM((depth, 1, rows), F32),
            pltpu.VMEM((plane, 1, rows), F32),
            pltpu.SemaphoreType.DMA,
            pltpu.SemaphoreType.DMA((count,)),
            pltpu.SemaphoreType.DMA,
            pltpu.SemaphoreType.DMA((depth,)),
            pltpu.SemaphoreType.DMA,
            pltpu.SemaphoreType.DMA((plane,)),
            pltpu.SemaphoreType.DMA,
            pltpu.SemaphoreType.DMA((depth,)),
            pltpu.SemaphoreType.DMA((plane,)),
        ],
        compiler_params=pltpu.CompilerParams(
            collective_id=0, has_side_effects=True, vmem_limit_bytes=48 * 1024 * 1024
        ),
    )(contexts, logged_actions.reshape(1, rows), policy_actions.T, rewards.reshape(1, rows))
    return results[0:NPOL].T, results[NPOL : 2 * NPOL].T, results[2 * NPOL, 0:NPOL]


def solution(mesh):
    rows_n, cols = mesh.shape["row"], mesh.shape["col"]
    depth = 4 if (cols // 2) % 4 == 0 else 1
    sizes = (rows_n, depth, cols // 2 // depth)
    placed = (
        P(("row", "col"), None),
        P(("row", "col")),
        P(("row", "col"), None),
        P(("row", "col")),
    )
    return jax.shard_map(
        functools.partial(on_device, sizes),
        mesh=mesh,
        in_specs=placed,
        out_specs=(P(("row", "col"), None), P(("row", "col"), None), P()),
        check_vma=False,
    )
```

```python
import functools
import math

import jax
import jax.numpy as jnp
from jax import lax
from jax.experimental import pallas as pl
from jax.experimental.pallas import tpu as pltpu
from jax.sharding import PartitionSpec as P

MESH = pl.DeviceIdType.MESH
F32 = jnp.float32
BF16 = jnp.bfloat16

NPOL = 8
NACT = 16
CATALOG = 131042
RIDGE = 0.1
STRIDE = 1009
PHASE = 0.37
TWO_PI = 2.0 * math.pi
META = 32


def loop(low, high, body):
    if isinstance(low, int) and isinstance(high, int) and high - low <= 4:
        for step in range(low, high):
            body(step)
    else:

        def wrapped(step, carried):
            body(step)
            return carried

        lax.fori_loop(low, high, wrapped, 0)


def cosine(turned, phase):
    whole = jnp.floor(turned.astype(F32) * (1.0 / CATALOG) + 0.5).astype(jnp.int32)
    rest = (turned - whole * CATALOG).astype(F32)
    turns = rest * (1.0 / CATALOG) + phase / TWO_PI
    turns = turns - jnp.floor(turns + 0.5)
    angle = TWO_PI * (0.25 - jnp.abs(turns))
    square = angle * angle
    series = -1.0 / 39916800.0
    for term in (362880.0, -5040.0, 120.0, -6.0, 1.0):
        series = series * square + 1.0 / term
    return series * angle


def features(chosen):
    twice = 2.0 * cosine(chosen * STRIDE, PHASE)
    before = cosine(chosen, 0.0)
    now = cosine(chosen * (1 + STRIDE), PHASE)
    scale = math.sqrt(2.0 / NACT)
    out = [jnp.full(chosen.shape, 1.0 / math.sqrt(NACT), F32)]
    for level in range(1, NACT):
        out.append(scale * now)
        before, now = now, twice * now - before
    return out


def rounded(parts):
    return jnp.concatenate(parts, axis=0).astype(BF16)


def dot(left, right, over=1):
    return lax.dot_general(left, right, (((over,), (0,)), ((), ())), preferred_element_type=F32)


def kernel(
    sizes,
    ctx_ref,
    logged_ref,
    policy_ref,
    reward_ref,
    results_ref,
    blocks,
    mate,
    part_out,
    part_in,
    image_out,
    image_in,
    near,
    sides,
    grams,
    logged_feat,
    total,
    near_sums,
    plane_sums,
    block_send,
    block_recv,
    pair_send,
    pair_recv,
    near_send,
    near_recv,
    side_send,
    side_recv,
    sum_send,
    sum_recv,
    sum_recv_plane,
):
    rows_n, depth, width = sizes
    half_groups = rows_n * width
    half = half_groups * depth
    plane = 2 * half_groups
    count = 2 * half
    rows, dims = ctx_ref.shape
    x = lax.axis_index("row")
    col = lax.axis_index("col")
    core = lax.rem(col, 2)
    y = lax.rem(lax.div(col, 2), width)
    z = lax.div(col, 2 * width)

    def inner_size(at_core):
        return width if rows_n == width else width + at_core * (rows_n - width)

    n1 = inner_size(core)
    n2 = inner_size(1 - core)
    i1 = y + core * (x - y)
    i2 = x + core * (y - x)
    own_group = i2 * n1 + i1
    own_plane = core * half_groups + own_group
    me = own_group * depth + z

    def device(first, second, at_z, at_core):
        at_x = second + at_core * (first - second)
        at_y = first + at_core * (second - first)
        return (at_x, (at_z * width + at_y) * 2 + at_core)

    def z_peer(step):
        return device(i1, i2, lax.rem(z + step, depth), core)

    def first_peer(step):
        return device(lax.rem(i1 + step, n1), i2, z, core)

    def second_peer(step):
        return device(i1, lax.rem(i2 + step, n2), z, core)

    def plane_peer(step):
        group = lax.rem(own_plane + step, plane)
        at_core = lax.div(group, half_groups)
        place = lax.rem(group, half_groups)
        inside = inner_size(at_core)
        return device(lax.rem(place, inside), lax.div(place, inside), z, at_core)

    def half_peer(step):
        place = lax.rem(own_group + step, half_groups)
        return device(lax.rem(place, n1), lax.div(place, n1), z, core)

    core_peer = (x, (z * width + y) * 2 + 1 - core)

    barrier = pltpu.get_barrier_semaphore()

    def greet(peer):
        pl.semaphore_signal(barrier, inc=1, device_id=peer, device_id_type=MESH)

    loop(1, depth, lambda step: greet(z_peer(step)))
    loop(1, plane, lambda step: greet(plane_peer(step)))

    own = ctx_ref[...]
    blocks[me, 0:rows, :] = own
    own_wide = own.astype(F32)
    own_squares = jnp.sum(own_wide * own_wide, axis=1, keepdims=True) * (1.0 / dims)
    here = lax.broadcasted_iota(jnp.int32, (rows, rows), 0)
    there = lax.broadcasted_iota(jnp.int32, (rows, rows), 1)
    squares_row = jnp.sum(jnp.where(here == there, own_squares, 0.0), axis=0, keepdims=True)
    place = lax.broadcasted_iota(jnp.int32, (META // 2, rows), 0)
    picks = jnp.where((place >= 9) & (place <= 11), -0.5 * dims, 0.0).astype(BF16)
    picks = jnp.concatenate([picks, picks], axis=1)

    def pieces(value):
        high = jnp.floor(value * (1.0 / 512.0) + 0.5)
        return high, value - 512.0 * high

    policy_high, policy_low = pieces(policy_ref[...].astype(F32))
    logged_high, logged_low = pieces(logged_ref[...].astype(F32))
    square_1 = squares_row.astype(BF16).astype(F32)
    square_2 = (squares_row - square_1).astype(BF16).astype(F32)
    square_3 = squares_row - square_1 - square_2
    meta = jnp.concatenate(
        [
            policy_high,
            policy_low,
            jnp.broadcast_to(logged_high, (8, rows)),
            logged_low,
            square_1,
            square_2,
            square_3,
            jnp.zeros((4, rows), F32),
        ],
        axis=0,
    )
    blocks[me, rows : rows + META, :] = meta.astype(BF16)
    total[...] = jnp.zeros_like(total)
    pl.semaphore_wait(barrier, (depth - 1) + (plane - 1))

    def remote(source, send_sem, recv_sem, peer):
        return pltpu.make_async_remote_copy(
            src_ref=source,
            dst_ref=source,
            send_sem=send_sem,
            recv_sem=recv_sem,
            device_id=peer,
            device_id_type=MESH,
        )

    def block_copy(index, peer):
        return remote(blocks.at[index], block_send, block_recv.at[index], peer)

    def to_first(index):
        loop(1, n1, lambda step: block_copy(index, first_peer(step)).start())

    def to_second(index):
        loop(1, n2, lambda step: block_copy(index, second_peer(step)).start())

    wide = depth * rows

    def meta_of(group):
        base = group * depth
        return jnp.concatenate(
            [blocks[base + k, rows : rows + META, :].astype(F32) for k in range(depth)], axis=1
        )

    def first_pass(group):
        base = group * depth
        meta_all = meta_of(group)
        policy = (meta_all[0:8] * 512.0 + meta_all[8:16]).astype(jnp.int32)
        others = jnp.concatenate([blocks[base + k, 0:rows, :] for k in range(depth)], axis=0)
        squares = jnp.concatenate(
            [blocks[base + k, rows + META // 2 : rows + META, :] for k in range(depth)], axis=1
        )
        inner = dot(others, pair_turned) + dot(squares, picks, 0)
        policy_feat = rounded(features(policy))
        gram = jnp.exp(inner * (2.0 / dims) - pair_squares).astype(BF16)
        grams[group] = gram
        total[...] += dot(policy_feat, gram)

    mate_copy = pltpu.make_async_remote_copy(
        src_ref=blocks.at[me],
        dst_ref=mate,
        send_sem=block_send,
        recv_sem=pair_recv.at[0],
        device_id=core_peer,
        device_id_type=MESH,
    )
    loop(1, depth, lambda step: block_copy(me, z_peer(step)).start())
    to_first(me)
    to_second(me)
    mate_copy.start()

    mate_copy.wait_recv()
    mate_wide = mate[0:rows, :].astype(F32)
    mate_meta = mate[rows : rows + META, :].astype(F32)
    mate_squares = mate_meta[25:26] + mate_meta[26:27] + mate_meta[27:28]
    mate_logged = (mate_meta[16:17] * 512.0 + mate_meta[24:25]).astype(jnp.int32)
    pair_turned = jnp.concatenate([own_wide.T, mate_wide.T], axis=1).astype(BF16)
    pair_squares = jnp.concatenate([squares_row, mate_squares], axis=1)
    pair_logged = jnp.concatenate([logged_ref[...], mate_logged], axis=1)

    def from_z(step):
        index = own_group * depth + lax.rem(z + step, depth)
        block_copy(index, core_peer).wait_recv()
        to_first(index)
        to_second(index)

    loop(1, depth, from_z)
    first_pass(own_group)

    def first_group(step):
        return i2 * n1 + lax.rem(i1 + step, n1)

    def from_first(step):
        group = first_group(step)

        def one(place):
            index = group * depth + place
            block_copy(index, core_peer).wait_recv()
            to_second(index)

        loop(0, depth, one)

    loop(1, n1, from_first)
    loop(1, n1, lambda step: first_pass(first_group(step)))

    def from_second(place):
        step = 1 + lax.div(place, n1)
        first = lax.rem(i1 + lax.rem(place, n1), n1)
        group = lax.rem(i2 + step, n2) * n1 + first
        loop(0, depth, lambda k: block_copy(group * depth + k, core_peer).wait_recv())
        first_pass(group)

    loop(0, (n2 - 1) * n1, from_second)

    factor = NACT / (rows * count)
    own_feat = [
        part.astype(BF16).astype(F32)
        for part in features(jnp.broadcast_to(pair_logged, (NPOL, 2 * rows)))
    ]

    def select():
        value = total[...]
        out = own_feat[0] * value[0:NPOL]
        for level in range(1, NACT):
            out += own_feat[level] * value[level * NPOL : (level + 1) * NPOL]
        return factor * out

    def show(group):
        meta_all = meta_of(group)
        shown = (meta_all[16:17] * 512.0 + meta_all[24:25]).astype(jnp.int32)
        logged_feat[group] = rounded(features(jnp.broadcast_to(shown, (NPOL, wide))))

    def pair_copy(source, target, at):
        return pltpu.make_async_remote_copy(
            src_ref=source,
            dst_ref=target,
            send_sem=pair_send.at[at],
            recv_sem=pair_recv.at[1 + at],
            device_id=core_peer,
            device_id_type=MESH,
        )

    def add_pair(mine, other):
        return (
            mine[:, 0:rows] + other[:, rows : 2 * rows],
            mine[:, rows : 2 * rows] + other[:, 0:rows],
        )

    part = select()
    part_out[...] = part
    part_copy = pair_copy(part_out, part_in, 0)
    part_copy.start()
    loop(0, half_groups // 2, show)
    part_copy.wait_recv()
    right_side, mate_side = add_pair(part, part_in[...])
    near[z] = right_side
    total[...] = jnp.zeros_like(total)

    def near_copy(place, peer):
        return remote(near.at[place], near_send, near_recv.at[place], peer)

    def side_copy(group, peer):
        return remote(sides.at[group], side_send, side_recv.at[group], peer)

    def second_pass(group):
        packed = sides[group].astype(F32)
        low = jnp.concatenate([packed[k * NPOL : (k + 1) * NPOL] for k in range(depth)], axis=1)
        feat = logged_feat[group].astype(F32)
        matched = (feat * jnp.concatenate([low] * NACT, axis=0)).astype(BF16)
        total[...] += dot(matched, grams[group])

    loop(1, depth, lambda step: near_copy(z, z_peer(step)).start())
    loop(half_groups // 2, half_groups, show)
    loop(1, depth, lambda step: near_copy(lax.rem(z + step, depth), core_peer).wait_recv())
    sides[own_group] = rounded([near[k] for k in range(depth)])
    loop(1, half_groups, lambda step: side_copy(own_group, half_peer(step)).start())
    second_pass(own_group)

    def from_plane(step):
        group = lax.rem(own_group + step, half_groups)
        side_copy(group, core_peer).wait_recv()
        second_pass(group)

    loop(1, half_groups, from_plane)
    image_part = select()
    image_out[...] = image_part
    image_copy = pair_copy(image_out, image_in, 1)
    image_copy.start()
    own_square = right_side * right_side
    curved = image_part[:, 0:rows] * right_side + image_part[:, rows : 2 * rows] * mate_side

    lane = lax.broadcasted_iota(jnp.int32, (NPOL, rows), 1)
    sub = lax.broadcasted_iota(jnp.int32, (NPOL, rows), 0)

    def to_row(value, offset):
        column = jnp.sum(value, axis=1, keepdims=True)
        return jnp.sum(jnp.where(lane == sub + offset, column, 0.0), axis=0, keepdims=True)

    partial = (
        to_row(own_square, 0)
        + to_row(curved + RIDGE * own_square, NPOL)
        + to_row(reward_ref[...] * right_side, 2 * NPOL)
    )

    def all_sum(value, slots, recv, at, size, peer_of):
        slots[at] = value
        loop(
            1,
            size,
            lambda step: remote(slots.at[at], sum_send, recv.at[at], peer_of(step)).start(),
        )

        def arrive(step):
            place = lax.rem(at + step, size)
            remote(slots.at[place], sum_send, recv.at[place], core_peer).wait_recv()

        loop(1, size, arrive)
        return jnp.sum(slots[...], axis=0)

    partial = all_sum(partial, near_sums, sum_recv, z, depth, z_peer)
    partial = all_sum(partial, plane_sums, sum_recv_plane, own_plane, plane, plane_peer)
    image_copy.wait_recv()
    image = add_pair(image_part, image_in[...])[0] + RIDGE * right_side

    def to_column(offset):
        spread_row = jnp.broadcast_to(partial, (NPOL, rows))
        return jnp.sum(jnp.where(lane == sub + offset, spread_row, 0.0), axis=1, keepdims=True)

    alpha = to_column(0) / to_column(NPOL)
    values_column = alpha * to_column(2 * NPOL) * (1.0 / (rows * count))
    values_row = jnp.sum(jnp.where(lane == sub, values_column, 0.0), axis=0, keepdims=True)
    results_ref[0:NPOL] = alpha * right_side
    results_ref[NPOL : 2 * NPOL] = right_side - alpha * image
    results_ref[2 * NPOL :] = jnp.broadcast_to(values_row, (NPOL, rows))

    remote(
        blocks, block_send, block_recv.at[0], core_peer
    ).wait_send()
    part_copy.wait_send()
    image_copy.wait_send()
    remote(near.at[pl.ds(0, depth - 1)], near_send, near_recv.at[0], core_peer).wait_send()
    remote(sides.at[pl.ds(0, half_groups - 1)], side_send, side_recv.at[0], core_peer).wait_send()
    remote(
        near_sums.at[pl.ds(0, depth - 1)], sum_send, sum_recv.at[0], core_peer
    ).wait_send()
    remote(
        plane_sums.at[pl.ds(0, plane - 1)], sum_send, sum_recv_plane.at[0], core_peer
    ).wait_send()


def on_device(sizes, contexts, logged_actions, policy_actions, rewards):
    rows_n, depth, width = sizes
    rows, dims = contexts.shape
    half_groups = rows_n * width
    plane = 2 * half_groups
    vmem = pl.BlockSpec(memory_space=pltpu.VMEM)
    results = pl.pallas_call(
        functools.partial(kernel, sizes),
        out_shape=jax.ShapeDtypeStruct((3 * NPOL, rows), F32),
        in_specs=[vmem] * 4,
        out_specs=vmem,
        scratch_shapes=[
            pltpu.VMEM((half_groups * depth, rows + META, dims), BF16),
            pltpu.VMEM((rows + META, dims), BF16),
            pltpu.VMEM((NPOL, 2 * rows), F32),
            pltpu.VMEM((NPOL, 2 * rows), F32),
            pltpu.VMEM((NPOL, 2 * rows), F32),
            pltpu.VMEM((NPOL, 2 * rows), F32),
            pltpu.VMEM((depth, NPOL, rows), F32),
            pltpu.VMEM((half_groups, depth * NPOL, rows), BF16),
            pltpu.VMEM((half_groups, depth * rows, 2 * rows), BF16),
            pltpu.VMEM((half_groups, NPOL * NACT, depth * rows), BF16),
            pltpu.VMEM((NPOL * NACT, 2 * rows), F32),
            pltpu.VMEM((depth, 1, rows), F32),
            pltpu.VMEM((plane, 1, rows), F32),
            pltpu.SemaphoreType.DMA,
            pltpu.SemaphoreType.DMA((half_groups * depth,)),
            pltpu.SemaphoreType.DMA((2,)),
            pltpu.SemaphoreType.DMA((3,)),
            pltpu.SemaphoreType.DMA,
            pltpu.SemaphoreType.DMA((depth,)),
            pltpu.SemaphoreType.DMA,
            pltpu.SemaphoreType.DMA((half_groups,)),
            pltpu.SemaphoreType.DMA,
            pltpu.SemaphoreType.DMA((depth,)),
            pltpu.SemaphoreType.DMA((plane,)),
        ],
        compiler_params=pltpu.CompilerParams(
            collective_id=0, has_side_effects=True, vmem_limit_bytes=48 * 1024 * 1024
        ),
    )(contexts, logged_actions.reshape(1, rows), policy_actions.T, rewards.reshape(1, rows))
    return results[0:NPOL].T, results[NPOL : 2 * NPOL].T, results[2 * NPOL, 0:NPOL]


def solution(mesh):
    rows_n, cols = mesh.shape["row"], mesh.shape["col"]
    depth = 4 if (cols // 2) % 4 == 0 else 1
    sizes = (rows_n, depth, cols // 2 // depth)
    placed = (
        P(("row", "col"), None),
        P(("row", "col")),
        P(("row", "col"), None),
        P(("row", "col")),
    )
    return jax.shard_map(
        functools.partial(on_device, sizes),
        mesh=mesh,
        in_specs=placed,
        out_specs=(P(("row", "col"), None), P(("row", "col"), None), P()),
        check_vma=False,
    )
```

```python
import functools
import math

import jax
import jax.numpy as jnp
from jax import lax
from jax.experimental import pallas as pl
from jax.experimental.pallas import tpu as pltpu
from jax.sharding import PartitionSpec as P

MESH = pl.DeviceIdType.MESH
F32 = jnp.float32
BF16 = jnp.bfloat16

NPOL = 8
NACT = 16
CATALOG = 131042
RIDGE = 0.1
STRIDE = 1009
PHASE = 0.37
TWO_PI = 2.0 * math.pi
META = 32


def loop(low, high, body):
    if isinstance(low, int) and isinstance(high, int) and high - low <= 4:
        for step in range(low, high):
            body(step)
    else:

        def wrapped(step, carried):
            body(step)
            return carried

        lax.fori_loop(low, high, wrapped, 0)


def cosine(turned, phase):
    whole = jnp.floor(turned.astype(F32) * (1.0 / CATALOG) + 0.5).astype(jnp.int32)
    rest = (turned - whole * CATALOG).astype(F32)
    turns = rest * (1.0 / CATALOG) + phase / TWO_PI
    turns = turns - jnp.floor(turns + 0.5)
    angle = TWO_PI * (0.25 - jnp.abs(turns))
    square = angle * angle
    series = -1.0 / 39916800.0
    for term in (362880.0, -5040.0, 120.0, -6.0, 1.0):
        series = series * square + 1.0 / term
    return series * angle


def features(chosen):
    twice = 2.0 * cosine(chosen * STRIDE, PHASE)
    before = cosine(chosen, 0.0)
    now = cosine(chosen * (1 + STRIDE), PHASE)
    scale = math.sqrt(2.0 / NACT)
    out = [jnp.full(chosen.shape, 1.0 / math.sqrt(NACT), F32)]
    for level in range(1, NACT):
        out.append(scale * now)
        before, now = now, twice * now - before
    return out


def rounded(parts):
    return jnp.concatenate(parts, axis=0).astype(BF16)


def dot(left, right, over=1):
    return lax.dot_general(left, right, (((over,), (0,)), ((), ())), preferred_element_type=F32)


def kernel(
    sizes,
    ctx_ref,
    logged_ref,
    policy_ref,
    reward_ref,
    results_ref,
    blocks,
    team,
    parts,
    team_sides,
    image_out,
    image_in,
    near,
    sides,
    grams,
    logged_feat,
    total,
    near_sums,
    plane_sums,
    block_send,
    block_recv,
    team_send,
    team_recv,
    part_send,
    part_recv,
    image_send,
    image_recv,
    near_send,
    near_recv,
    side_send,
    side_recv,
    sum_send,
    sum_recv,
    sum_recv_plane,
):
    rows_n, depth, width = sizes
    members = 2 * rows_n
    plane = members * width
    count = plane * depth
    rows, dims = ctx_ref.shape
    x = lax.axis_index("row")
    col = lax.axis_index("col")
    core = lax.rem(col, 2)
    y = lax.rem(lax.div(col, 2), width)
    z = lax.div(col, 2 * width)

    member = x * 2 + core
    own_plane = y * members + member
    me = y * depth + z

    def device(at_member, at_y, at_z):
        return (
            lax.div(at_member, 2),
            (at_z * width + at_y) * 2 + lax.rem(at_member, 2),
        )

    def z_peer(step):
        return device(member, y, lax.rem(z + step, depth))

    def y_peer(step):
        return device(member, lax.rem(y + step, width), z)

    def team_peer(step):
        return device(lax.rem(member + step, members), y, z)

    def plane_peer(step):
        place = lax.rem(own_plane + step, plane)
        return device(lax.rem(place, members), lax.div(place, members), z)

    any_peer = team_peer(1)

    barrier = pltpu.get_barrier_semaphore()

    def greet(peer):
        pl.semaphore_signal(barrier, inc=1, device_id=peer, device_id_type=MESH)

    loop(1, depth, lambda step: greet(z_peer(step)))
    loop(1, plane, lambda step: greet(plane_peer(step)))

    own = ctx_ref[...]
    blocks[me, 0:rows, :] = own
    team[member, 0:rows, :] = own
    own_wide = own.astype(F32)
    own_squares = jnp.sum(own_wide * own_wide, axis=1, keepdims=True) * (1.0 / dims)
    here = lax.broadcasted_iota(jnp.int32, (rows, rows), 0)
    there = lax.broadcasted_iota(jnp.int32, (rows, rows), 1)
    squares_row = jnp.sum(jnp.where(here == there, own_squares, 0.0), axis=0, keepdims=True)
    place = lax.broadcasted_iota(jnp.int32, (META // 2, rows), 0)
    picks = jnp.where((place >= 9) & (place <= 11), -0.5 * dims, 0.0).astype(BF16)
    picks = jnp.concatenate([picks] * members, axis=1)

    def pieces(value):
        high = jnp.floor(value * (1.0 / 512.0) + 0.5)
        return high, value - 512.0 * high

    policy_high, policy_low = pieces(policy_ref[...].astype(F32))
    logged_high, logged_low = pieces(logged_ref[...].astype(F32))
    square_1 = squares_row.astype(BF16).astype(F32)
    square_2 = (squares_row - square_1).astype(BF16).astype(F32)
    square_3 = squares_row - square_1 - square_2
    meta = jnp.concatenate(
        [
            policy_high,
            policy_low,
            jnp.broadcast_to(logged_high, (8, rows)),
            logged_low,
            square_1,
            square_2,
            square_3,
            jnp.zeros((4, rows), F32),
        ],
        axis=0,
    )
    blocks[me, rows : rows + META, :] = meta.astype(BF16)
    team[member, rows : rows + META, :] = meta.astype(BF16)
    total[...] = jnp.zeros_like(total)
    pl.semaphore_wait(barrier, (depth - 1) + (plane - 1))

    def remote(source, send_sem, recv_sem, peer):
        return pltpu.make_async_remote_copy(
            src_ref=source,
            dst_ref=source,
            send_sem=send_sem,
            recv_sem=recv_sem,
            device_id=peer,
            device_id_type=MESH,
        )

    def block_copy(index, peer):
        return remote(blocks.at[index], block_send, block_recv.at[index], peer)

    def to_y(index):
        loop(1, width, lambda step: block_copy(index, y_peer(step)).start())

    def team_copy(place, peer):
        return remote(team.at[place], team_send, team_recv.at[place], peer)

    wide = depth * rows

    def meta_of(group):
        base = group * depth
        return jnp.concatenate(
            [blocks[base + k, rows : rows + META, :].astype(F32) for k in range(depth)], axis=1
        )

    def first_pass(group):
        base = group * depth
        meta_all = meta_of(group)
        policy = (meta_all[0:8] * 512.0 + meta_all[8:16]).astype(jnp.int32)
        others = jnp.concatenate([blocks[base + k, 0:rows, :] for k in range(depth)], axis=0)
        squares = jnp.concatenate(
            [blocks[base + k, rows + META // 2 : rows + META, :] for k in range(depth)], axis=1
        )
        inner = dot(others, team_turned) + dot(squares, picks, 0)
        policy_feat = rounded(features(policy))
        gram = jnp.exp(inner * (2.0 / dims) - team_squares).astype(BF16)
        grams[group] = gram
        total[...] += dot(policy_feat, gram)

    loop(1, depth, lambda step: block_copy(me, z_peer(step)).start())
    to_y(me)
    loop(1, members, lambda step: team_copy(member, team_peer(step)).start())

    def from_z(step):
        index = y * depth + lax.rem(z + step, depth)
        block_copy(index, any_peer).wait_recv()
        to_y(index)

    loop(1, members, lambda k: team_copy(lax.rem(member + k, members), any_peer).wait_recv())
    turned_parts, square_parts, logged_parts = [], [], []
    for k in range(members):
        row_meta = team[k, rows : rows + META, :].astype(F32)
        turned_parts.append(team[k, 0:rows, :].astype(F32).T)
        square_parts.append(row_meta[25:26] + row_meta[26:27] + row_meta[27:28])
        logged_parts.append((row_meta[16:17] * 512.0 + row_meta[24:25]).astype(jnp.int32))
    team_turned = jnp.concatenate(turned_parts, axis=1).astype(BF16)
    team_squares = jnp.concatenate(square_parts, axis=1)
    team_logged = jnp.concatenate(logged_parts, axis=1)

    loop(1, depth, from_z)
    first_pass(y)

    def from_y(step):
        group = lax.rem(y + step, width)
        loop(0, depth, lambda k: block_copy(group * depth + k, any_peer).wait_recv())
        first_pass(group)

    loop(1, width, from_y)

    factor = NACT / (rows * count)
    own_feat = [
        part.astype(BF16).astype(F32)
        for part in features(jnp.broadcast_to(team_logged, (NPOL, members * rows)))
    ]

    def select():
        value = total[...]
        out = own_feat[0] * value[0:NPOL]
        for level in range(1, NACT):
            out += own_feat[level] * value[level * NPOL : (level + 1) * NPOL]
        return factor * out

    def show(group):
        meta_all = meta_of(group)
        shown = (meta_all[16:17] * 512.0 + meta_all[24:25]).astype(jnp.int32)
        logged_feat[group] = rounded(features(jnp.broadcast_to(shown, (NPOL, wide))))

    def part_copy(place, peer):
        return remote(parts.at[place], part_send, part_recv.at[place], peer)

    parts[member] = select()
    loop(1, members, lambda step: part_copy(member, team_peer(step)).start())
    loop(0, width, show)
    loop(1, members, lambda k: part_copy(lax.rem(member + k, members), any_peer).wait_recv())
    all_sides = jnp.sum(parts[...], axis=0)
    for k in range(members):
        team_sides[k] = all_sides[:, k * rows : (k + 1) * rows]
    right_side = team_sides[member]
    near[z] = right_side
    total[...] = jnp.zeros_like(total)

    def near_copy(place, peer):
        return remote(near.at[place], near_send, near_recv.at[place], peer)

    def side_copy(group, peer):
        return remote(sides.at[group], side_send, side_recv.at[group], peer)

    def second_pass(group):
        packed = sides[group].astype(F32)
        low = jnp.concatenate([packed[k * NPOL : (k + 1) * NPOL] for k in range(depth)], axis=1)
        feat = logged_feat[group].astype(F32)
        matched = (feat * jnp.concatenate([low] * NACT, axis=0)).astype(BF16)
        total[...] += dot(matched, grams[group])

    loop(1, depth, lambda step: near_copy(z, z_peer(step)).start())
    loop(1, depth, lambda step: near_copy(lax.rem(z + step, depth), any_peer).wait_recv())
    sides[y] = rounded([near[k] for k in range(depth)])
    loop(1, width, lambda step: side_copy(y, y_peer(step)).start())
    second_pass(y)

    def from_plane(step):
        group = lax.rem(y + step, width)
        side_copy(group, any_peer).wait_recv()
        second_pass(group)

    loop(1, width, from_plane)
    image_part = select()
    for k in range(members):
        image_out[k] = image_part[:, k * rows : (k + 1) * rows]
    image_in[member] = image_out[member]

    def image_copy(source, target, peer):
        return pltpu.make_async_remote_copy(
            src_ref=image_out.at[source],
            dst_ref=image_in.at[target],
            send_sem=image_send,
            recv_sem=image_recv.at[target],
            device_id=peer,
            device_id_type=MESH,
        )

    def send_image(step):
        image_copy(lax.rem(member + step, members), member, team_peer(step)).start()

    loop(1, members, send_image)
    own_square = right_side * right_side
    curved = image_out[0] * team_sides[0]
    for k in range(1, members):
        curved += image_out[k] * team_sides[k]

    lane = lax.broadcasted_iota(jnp.int32, (NPOL, rows), 1)
    sub = lax.broadcasted_iota(jnp.int32, (NPOL, rows), 0)

    def to_row(value, offset):
        column = jnp.sum(value, axis=1, keepdims=True)
        return jnp.sum(jnp.where(lane == sub + offset, column, 0.0), axis=0, keepdims=True)

    partial = (
        to_row(own_square, 0)
        + to_row(curved + RIDGE * own_square, NPOL)
        + to_row(reward_ref[...] * right_side, 2 * NPOL)
    )

    def all_sum(value, slots, recv, at, size, peer_of):
        slots[at] = value
        loop(
            1,
            size,
            lambda step: remote(slots.at[at], sum_send, recv.at[at], peer_of(step)).start(),
        )

        def arrive(step):
            place = lax.rem(at + step, size)
            remote(slots.at[place], sum_send, recv.at[place], any_peer).wait_recv()

        loop(1, size, arrive)
        return jnp.sum(slots[...], axis=0)

    partial = all_sum(partial, near_sums, sum_recv, z, depth, z_peer)
    partial = all_sum(partial, plane_sums, sum_recv_plane, own_plane, plane, plane_peer)

    def image_arrives(step):
        place = lax.rem(member + step, members)
        image_copy(place, place, any_peer).wait_recv()

    loop(1, members, image_arrives)
    image = jnp.sum(image_in[...], axis=0) + RIDGE * right_side

    def to_column(offset):
        spread_row = jnp.broadcast_to(partial, (NPOL, rows))
        return jnp.sum(jnp.where(lane == sub + offset, spread_row, 0.0), axis=1, keepdims=True)

    alpha = to_column(0) / to_column(NPOL)
    values_column = alpha * to_column(2 * NPOL) * (1.0 / (rows * count))
    values_row = jnp.sum(jnp.where(lane == sub, values_column, 0.0), axis=0, keepdims=True)
    results_ref[0:NPOL] = alpha * right_side
    results_ref[NPOL : 2 * NPOL] = right_side - alpha * image
    results_ref[2 * NPOL :] = jnp.broadcast_to(values_row, (NPOL, rows))

    blocks_sent = blocks.at[pl.ds(0, depth * width - 1)]
    remote(blocks_sent, block_send, block_recv.at[0], any_peer).wait_send()
    others = pl.ds(0, members - 1)
    remote(team.at[others], team_send, team_recv.at[0], any_peer).wait_send()
    remote(parts.at[others], part_send, part_recv.at[0], any_peer).wait_send()
    remote(image_out.at[others], image_send, image_recv.at[0], any_peer).wait_send()
    remote(near.at[pl.ds(0, depth - 1)], near_send, near_recv.at[0], any_peer).wait_send()
    remote(sides.at[pl.ds(0, width - 1)], side_send, side_recv.at[0], any_peer).wait_send()
    remote(
        near_sums.at[pl.ds(0, depth - 1)], sum_send, sum_recv.at[0], any_peer
    ).wait_send()
    remote(
        plane_sums.at[pl.ds(0, plane - 1)], sum_send, sum_recv_plane.at[0], any_peer
    ).wait_send()


def on_device(sizes, contexts, logged_actions, policy_actions, rewards):
    rows_n, depth, width = sizes
    rows, dims = contexts.shape
    members = 2 * rows_n
    plane = members * width
    vmem = pl.BlockSpec(memory_space=pltpu.VMEM)
    results = pl.pallas_call(
        functools.partial(kernel, sizes),
        out_shape=jax.ShapeDtypeStruct((3 * NPOL, rows), F32),
        in_specs=[vmem] * 4,
        out_specs=vmem,
        scratch_shapes=[
            pltpu.VMEM((width * depth, rows + META, dims), BF16),
            pltpu.VMEM((members, rows + META, dims), BF16),
            pltpu.VMEM((members, NPOL, members * rows), F32),
            pltpu.VMEM((members, NPOL, rows), F32),
            pltpu.VMEM((members, NPOL, rows), F32),
            pltpu.VMEM((members, NPOL, rows), F32),
            pltpu.VMEM((depth, NPOL, rows), F32),
            pltpu.VMEM((width, depth * NPOL, rows), BF16),
            pltpu.VMEM((width, depth * rows, members * rows), BF16),
            pltpu.VMEM((width, NPOL * NACT, depth * rows), BF16),
            pltpu.VMEM((NPOL * NACT, members * rows), F32),
            pltpu.VMEM((depth, 1, rows), F32),
            pltpu.VMEM((plane, 1, rows), F32),
            pltpu.SemaphoreType.DMA,
            pltpu.SemaphoreType.DMA((width * depth,)),
            pltpu.SemaphoreType.DMA,
            pltpu.SemaphoreType.DMA((members,)),
            pltpu.SemaphoreType.DMA,
            pltpu.SemaphoreType.DMA((members,)),
            pltpu.SemaphoreType.DMA,
            pltpu.SemaphoreType.DMA((members,)),
            pltpu.SemaphoreType.DMA,
            pltpu.SemaphoreType.DMA((depth,)),
            pltpu.SemaphoreType.DMA,
            pltpu.SemaphoreType.DMA((width,)),
            pltpu.SemaphoreType.DMA,
            pltpu.SemaphoreType.DMA((depth,)),
            pltpu.SemaphoreType.DMA((plane,)),
        ],
        compiler_params=pltpu.CompilerParams(
            collective_id=0, has_side_effects=True, vmem_limit_bytes=48 * 1024 * 1024
        ),
    )(contexts, logged_actions.reshape(1, rows), policy_actions.T, rewards.reshape(1, rows))
    return results[0:NPOL].T, results[NPOL : 2 * NPOL].T, results[2 * NPOL, 0:NPOL]


def solution(mesh):
    rows_n, cols = mesh.shape["row"], mesh.shape["col"]
    depth = 4 if (cols // 2) % 4 == 0 else 1
    sizes = (rows_n, depth, cols // 2 // depth)
    placed = (
        P(("row", "col"), None),
        P(("row", "col")),
        P(("row", "col"), None),
        P(("row", "col")),
    )
    return jax.shard_map(
        functools.partial(on_device, sizes),
        mesh=mesh,
        in_specs=placed,
        out_specs=(P(("row", "col"), None), P(("row", "col"), None), P()),
        check_vma=False,
    )
```

```python
import functools
import math

import jax
import jax.numpy as jnp
from jax import lax
from jax.experimental import pallas as pl
from jax.experimental.pallas import tpu as pltpu
from jax.sharding import PartitionSpec as P

MESH = pl.DeviceIdType.MESH
F32 = jnp.float32
BF16 = jnp.bfloat16

NPOL = 8
NACT = 16
CATALOG = 131042
RIDGE = 0.1
STRIDE = 1009
PHASE = 0.37
TWO_PI = 2.0 * math.pi
META = 32


def loop(low, high, body):
    if isinstance(low, int) and isinstance(high, int) and high - low <= 4:
        for step in range(low, high):
            body(step)
    else:

        def wrapped(step, carried):
            body(step)
            return carried

        lax.fori_loop(low, high, wrapped, 0)


def cosine(turned, phase):
    whole = jnp.floor(turned.astype(F32) * (1.0 / CATALOG) + 0.5).astype(jnp.int32)
    rest = (turned - whole * CATALOG).astype(F32)
    turns = rest * (1.0 / CATALOG) + phase / TWO_PI
    turns = turns - jnp.floor(turns + 0.5)
    angle = TWO_PI * (0.25 - jnp.abs(turns))
    square = angle * angle
    series = -1.0 / 39916800.0
    for term in (362880.0, -5040.0, 120.0, -6.0, 1.0):
        series = series * square + 1.0 / term
    return series * angle


def features(chosen):
    twice = 2.0 * cosine(chosen * STRIDE, PHASE)
    before = cosine(chosen, 0.0)
    now = cosine(chosen * (1 + STRIDE), PHASE)
    scale = math.sqrt(2.0 / NACT)
    out = [jnp.full(chosen.shape, 1.0 / math.sqrt(NACT), F32)]
    for level in range(1, NACT):
        out.append(scale * now)
        before, now = now, twice * now - before
    return out


def rounded(parts):
    return jnp.concatenate(parts, axis=0).astype(BF16)


def dot(left, right, over=1):
    return lax.dot_general(left, right, (((over,), (0,)), ((), ())), preferred_element_type=F32)


def kernel(
    sizes,
    ctx_ref,
    logged_ref,
    policy_ref,
    reward_ref,
    results_ref,
    blocks,
    team,
    parts,
    team_sides,
    image_out,
    image_in,
    near,
    sides,
    grams,
    logged_feat,
    total,
    near_sums,
    plane_sums,
    block_send,
    block_recv,
    team_send,
    team_recv,
    part_send,
    part_recv,
    image_send,
    image_recv,
    near_send,
    near_recv,
    side_send,
    side_recv,
    sum_send,
    sum_recv,
    sum_recv_plane,
):
    rows_n, depth, full, fold = sizes
    width = full // fold
    members = 2 * rows_n * fold
    plane = members * width
    count = plane * depth
    rows, dims = ctx_ref.shape
    x = lax.axis_index("row")
    col = lax.axis_index("col")
    core = lax.rem(col, 2)
    at_full = lax.rem(lax.div(col, 2), full)
    y = lax.div(at_full, fold)
    z = lax.div(col, 2 * full)

    member = (x * fold + lax.rem(at_full, fold)) * 2 + core
    own_plane = y * members + member
    me = y * depth + z

    def device(at_member, at_y, at_z):
        place = lax.div(at_member, 2)
        line = at_y * fold + lax.rem(place, fold)
        return (lax.div(place, fold), (at_z * full + line) * 2 + lax.rem(at_member, 2))

    def z_peer(step):
        return device(member, y, lax.rem(z + step, depth))

    def y_peer(step):
        return device(member, lax.rem(y + step, width), z)

    def team_peer(step):
        return device(lax.rem(member + step, members), y, z)

    def plane_peer(step):
        place = lax.rem(own_plane + step, plane)
        return device(lax.rem(place, members), lax.div(place, members), z)

    any_peer = team_peer(1)

    barrier = pltpu.get_barrier_semaphore()

    def greet(peer):
        pl.semaphore_signal(barrier, inc=1, device_id=peer, device_id_type=MESH)

    loop(1, depth, lambda step: greet(z_peer(step)))
    loop(1, plane, lambda step: greet(plane_peer(step)))

    own = ctx_ref[...]
    blocks[me, 0:rows, :] = own
    team[member, 0:rows, :] = own
    own_wide = own.astype(F32)
    own_squares = jnp.sum(own_wide * own_wide, axis=1, keepdims=True) * (1.0 / dims)
    here = lax.broadcasted_iota(jnp.int32, (rows, rows), 0)
    there = lax.broadcasted_iota(jnp.int32, (rows, rows), 1)
    squares_row = jnp.sum(jnp.where(here == there, own_squares, 0.0), axis=0, keepdims=True)
    place = lax.broadcasted_iota(jnp.int32, (META // 2, rows), 0)
    picks = jnp.where((place >= 9) & (place <= 11), -0.5 * dims, 0.0).astype(BF16)
    picks = jnp.concatenate([picks] * members, axis=1)

    def pieces(value):
        high = jnp.floor(value * (1.0 / 512.0) + 0.5)
        return high, value - 512.0 * high

    policy_high, policy_low = pieces(policy_ref[...].astype(F32))
    logged_high, logged_low = pieces(logged_ref[...].astype(F32))
    square_1 = squares_row.astype(BF16).astype(F32)
    square_2 = (squares_row - square_1).astype(BF16).astype(F32)
    square_3 = squares_row - square_1 - square_2
    meta = jnp.concatenate(
        [
            policy_high,
            policy_low,
            jnp.broadcast_to(logged_high, (8, rows)),
            logged_low,
            square_1,
            square_2,
            square_3,
            jnp.zeros((4, rows), F32),
        ],
        axis=0,
    )
    blocks[me, rows : rows + META, :] = meta.astype(BF16)
    team[member, rows : rows + META, :] = meta.astype(BF16)
    total[...] = jnp.zeros_like(total)
    pl.semaphore_wait(barrier, (depth - 1) + (plane - 1))

    def remote(source, send_sem, recv_sem, peer):
        return pltpu.make_async_remote_copy(
            src_ref=source,
            dst_ref=source,
            send_sem=send_sem,
            recv_sem=recv_sem,
            device_id=peer,
            device_id_type=MESH,
        )

    def block_copy(index, peer):
        return remote(blocks.at[index], block_send, block_recv.at[index], peer)

    def to_y(index):
        loop(1, width, lambda step: block_copy(index, y_peer(step)).start())

    def team_copy(place, peer):
        return remote(team.at[place], team_send, team_recv.at[place], peer)

    wide = depth * rows

    def meta_of(group):
        base = group * depth
        return jnp.concatenate(
            [blocks[base + k, rows : rows + META, :].astype(F32) for k in range(depth)], axis=1
        )

    def first_pass(group):
        base = group * depth
        meta_all = meta_of(group)
        policy = (meta_all[0:8] * 512.0 + meta_all[8:16]).astype(jnp.int32)
        others = jnp.concatenate([blocks[base + k, 0:rows, :] for k in range(depth)], axis=0)
        squares = jnp.concatenate(
            [blocks[base + k, rows + META // 2 : rows + META, :] for k in range(depth)], axis=1
        )
        inner = dot(others, team_turned) + dot(squares, picks, 0)
        policy_feat = rounded(features(policy))
        gram = jnp.exp(inner * (2.0 / dims) - team_squares).astype(BF16)
        grams[group] = gram
        total[...] += dot(policy_feat, gram)

    loop(1, depth, lambda step: block_copy(me, z_peer(step)).start())
    to_y(me)
    loop(1, members, lambda step: team_copy(member, team_peer(step)).start())

    def from_z(step):
        index = y * depth + lax.rem(z + step, depth)
        block_copy(index, any_peer).wait_recv()
        to_y(index)

    loop(1, members, lambda k: team_copy(lax.rem(member + k, members), any_peer).wait_recv())
    turned_parts, square_parts, logged_parts = [], [], []
    for k in range(members):
        row_meta = team[k, rows : rows + META, :].astype(F32)
        turned_parts.append(team[k, 0:rows, :].astype(F32).T)
        square_parts.append(row_meta[25:26] + row_meta[26:27] + row_meta[27:28])
        logged_parts.append((row_meta[16:17] * 512.0 + row_meta[24:25]).astype(jnp.int32))
    team_turned = jnp.concatenate(turned_parts, axis=1).astype(BF16)
    team_squares = jnp.concatenate(square_parts, axis=1)
    team_logged = jnp.concatenate(logged_parts, axis=1)

    loop(1, depth, from_z)
    first_pass(y)

    def from_y(step):
        group = lax.rem(y + step, width)
        loop(0, depth, lambda k: block_copy(group * depth + k, any_peer).wait_recv())
        first_pass(group)

    loop(1, width, from_y)

    factor = NACT / (rows * count)
    own_feat = [
        part.astype(BF16).astype(F32)
        for part in features(jnp.broadcast_to(team_logged, (NPOL, members * rows)))
    ]

    def select():
        value = total[...]
        out = own_feat[0] * value[0:NPOL]
        for level in range(1, NACT):
            out += own_feat[level] * value[level * NPOL : (level + 1) * NPOL]
        return factor * out

    def show(group):
        meta_all = meta_of(group)
        shown = (meta_all[16:17] * 512.0 + meta_all[24:25]).astype(jnp.int32)
        logged_feat[group] = rounded(features(jnp.broadcast_to(shown, (NPOL, wide))))

    def part_copy(place, peer):
        return remote(parts.at[place], part_send, part_recv.at[place], peer)

    parts[member] = select()
    loop(1, members, lambda step: part_copy(member, team_peer(step)).start())
    loop(0, width, show)
    loop(1, members, lambda k: part_copy(lax.rem(member + k, members), any_peer).wait_recv())
    all_sides = jnp.sum(parts[...], axis=0)
    for k in range(members):
        team_sides[k] = all_sides[:, k * rows : (k + 1) * rows]
    right_side = team_sides[member]
    near[z] = right_side
    total[...] = jnp.zeros_like(total)

    def near_copy(place, peer):
        return remote(near.at[place], near_send, near_recv.at[place], peer)

    def side_copy(group, peer):
        return remote(sides.at[group], side_send, side_recv.at[group], peer)

    def second_pass(group):
        packed = sides[group].astype(F32)
        low = jnp.concatenate([packed[k * NPOL : (k + 1) * NPOL] for k in range(depth)], axis=1)
        feat = logged_feat[group].astype(F32)
        matched = (feat * jnp.concatenate([low] * NACT, axis=0)).astype(BF16)
        total[...] += dot(matched, grams[group])

    loop(1, depth, lambda step: near_copy(z, z_peer(step)).start())
    loop(1, depth, lambda step: near_copy(lax.rem(z + step, depth), any_peer).wait_recv())
    sides[y] = rounded([near[k] for k in range(depth)])
    loop(1, width, lambda step: side_copy(y, y_peer(step)).start())
    second_pass(y)

    def from_plane(step):
        group = lax.rem(y + step, width)
        side_copy(group, any_peer).wait_recv()
        second_pass(group)

    loop(1, width, from_plane)
    image_part = select()
    for k in range(members):
        image_out[k] = image_part[:, k * rows : (k + 1) * rows]
    image_in[member] = image_out[member]

    def image_copy(source, target, peer):
        return pltpu.make_async_remote_copy(
            src_ref=image_out.at[source],
            dst_ref=image_in.at[target],
            send_sem=image_send,
            recv_sem=image_recv.at[target],
            device_id=peer,
            device_id_type=MESH,
        )

    def send_image(step):
        image_copy(lax.rem(member + step, members), member, team_peer(step)).start()

    loop(1, members, send_image)
    own_square = right_side * right_side
    curved = image_out[0] * team_sides[0]
    for k in range(1, members):
        curved += image_out[k] * team_sides[k]

    lane = lax.broadcasted_iota(jnp.int32, (NPOL, rows), 1)
    sub = lax.broadcasted_iota(jnp.int32, (NPOL, rows), 0)

    def to_row(value, offset):
        column = jnp.sum(value, axis=1, keepdims=True)
        return jnp.sum(jnp.where(lane == sub + offset, column, 0.0), axis=0, keepdims=True)

    partial = (
        to_row(own_square, 0)
        + to_row(curved + RIDGE * own_square, NPOL)
        + to_row(reward_ref[...] * right_side, 2 * NPOL)
    )

    def all_sum(value, slots, recv, at, size, peer_of):
        slots[at] = value
        loop(
            1,
            size,
            lambda step: remote(slots.at[at], sum_send, recv.at[at], peer_of(step)).start(),
        )

        def arrive(step):
            place = lax.rem(at + step, size)
            remote(slots.at[place], sum_send, recv.at[place], any_peer).wait_recv()

        loop(1, size, arrive)
        return jnp.sum(slots[...], axis=0)

    partial = all_sum(partial, near_sums, sum_recv, z, depth, z_peer)
    partial = all_sum(partial, plane_sums, sum_recv_plane, own_plane, plane, plane_peer)

    def image_arrives(step):
        place = lax.rem(member + step, members)
        image_copy(place, place, any_peer).wait_recv()

    loop(1, members, image_arrives)
    image = jnp.sum(image_in[...], axis=0) + RIDGE * right_side

    def to_column(offset):
        spread_row = jnp.broadcast_to(partial, (NPOL, rows))
        return jnp.sum(jnp.where(lane == sub + offset, spread_row, 0.0), axis=1, keepdims=True)

    alpha = to_column(0) / to_column(NPOL)
    values_column = alpha * to_column(2 * NPOL) * (1.0 / (rows * count))
    values_row = jnp.sum(jnp.where(lane == sub, values_column, 0.0), axis=0, keepdims=True)
    results_ref[0:NPOL] = alpha * right_side
    results_ref[NPOL : 2 * NPOL] = right_side - alpha * image
    results_ref[2 * NPOL :] = jnp.broadcast_to(values_row, (NPOL, rows))

    blocks_sent = blocks.at[pl.ds(0, depth * width - 1)]
    remote(blocks_sent, block_send, block_recv.at[0], any_peer).wait_send()
    others = pl.ds(0, members - 1)
    remote(team.at[others], team_send, team_recv.at[0], any_peer).wait_send()
    remote(parts.at[others], part_send, part_recv.at[0], any_peer).wait_send()
    remote(image_out.at[others], image_send, image_recv.at[0], any_peer).wait_send()
    remote(near.at[pl.ds(0, depth - 1)], near_send, near_recv.at[0], any_peer).wait_send()
    if width > 1:
        sides_sent = sides.at[pl.ds(0, width - 1)]
        remote(sides_sent, side_send, side_recv.at[0], any_peer).wait_send()
    remote(
        near_sums.at[pl.ds(0, depth - 1)], sum_send, sum_recv.at[0], any_peer
    ).wait_send()
    remote(
        plane_sums.at[pl.ds(0, plane - 1)], sum_send, sum_recv_plane.at[0], any_peer
    ).wait_send()


def on_device(sizes, contexts, logged_actions, policy_actions, rewards):
    rows_n, depth, full, fold = sizes
    width = full // fold
    rows, dims = contexts.shape
    members = 2 * rows_n * fold
    plane = members * width
    vmem = pl.BlockSpec(memory_space=pltpu.VMEM)
    results = pl.pallas_call(
        functools.partial(kernel, sizes),
        out_shape=jax.ShapeDtypeStruct((3 * NPOL, rows), F32),
        in_specs=[vmem] * 4,
        out_specs=vmem,
        scratch_shapes=[
            pltpu.VMEM((width * depth, rows + META, dims), BF16),
            pltpu.VMEM((members, rows + META, dims), BF16),
            pltpu.VMEM((members, NPOL, members * rows), F32),
            pltpu.VMEM((members, NPOL, rows), F32),
            pltpu.VMEM((members, NPOL, rows), F32),
            pltpu.VMEM((members, NPOL, rows), F32),
            pltpu.VMEM((depth, NPOL, rows), F32),
            pltpu.VMEM((width, depth * NPOL, rows), BF16),
            pltpu.VMEM((width, depth * rows, members * rows), BF16),
            pltpu.VMEM((width, NPOL * NACT, depth * rows), BF16),
            pltpu.VMEM((NPOL * NACT, members * rows), F32),
            pltpu.VMEM((depth, 1, rows), F32),
            pltpu.VMEM((plane, 1, rows), F32),
            pltpu.SemaphoreType.DMA,
            pltpu.SemaphoreType.DMA((width * depth,)),
            pltpu.SemaphoreType.DMA,
            pltpu.SemaphoreType.DMA((members,)),
            pltpu.SemaphoreType.DMA,
            pltpu.SemaphoreType.DMA((members,)),
            pltpu.SemaphoreType.DMA,
            pltpu.SemaphoreType.DMA((members,)),
            pltpu.SemaphoreType.DMA,
            pltpu.SemaphoreType.DMA((depth,)),
            pltpu.SemaphoreType.DMA,
            pltpu.SemaphoreType.DMA((width,)),
            pltpu.SemaphoreType.DMA,
            pltpu.SemaphoreType.DMA((depth,)),
            pltpu.SemaphoreType.DMA((plane,)),
        ],
        compiler_params=pltpu.CompilerParams(
            collective_id=0, has_side_effects=True, vmem_limit_bytes=48 * 1024 * 1024
        ),
    )(contexts, logged_actions.reshape(1, rows), policy_actions.T, rewards.reshape(1, rows))
    return results[0:NPOL].T, results[NPOL : 2 * NPOL].T, results[2 * NPOL, 0:NPOL]


def solution(mesh):
    rows_n, cols = mesh.shape["row"], mesh.shape["col"]
    depth = 4 if (cols // 2) % 4 == 0 else 1
    width = cols // 2 // depth
    fold = width if rows_n * width <= 4 else 1
    sizes = (rows_n, depth, width, fold)
    placed = (
        P(("row", "col"), None),
        P(("row", "col")),
        P(("row", "col"), None),
        P(("row", "col")),
    )
    return jax.shard_map(
        functools.partial(on_device, sizes),
        mesh=mesh,
        in_specs=placed,
        out_specs=(P(("row", "col"), None), P(("row", "col"), None), P()),
        check_vma=False,
    )
```
